512 devices in a mesh: ctx: 64 (over y, z_lo, core), tp: 8 (over x, z_hi).
Axes of the slice: x: 4, y: 8, z: 8 (z_hi: 2, z_lo: 4; z = z_hi * 4 + z_lo), core: 2. Of those that a mesh axis runs over, the one named last changes fastest.
Arguments:
- queries: bfloat16 [2, 8192, 8192], P(None, 'ctx', 'tp'), may hold values from -8 to 8
- keys: bfloat16 [2, 8192, 512], P(None, 'ctx'), may hold values from -8 to 8
- values: bfloat16 [2, 8192, 512], P(None, 'ctx'), may hold values from -6 to 6
- doc_lengths: int32 [16], replicated, may hold values from 1 to 4096, as said below
Outputs:
- attended: bfloat16 [2, 8192, 8192], P(None, 'ctx', 'tp')
- lse_gap: float32 [8192], P('ctx')
The draws below stay inside these ranges and needn't reach their ends.
Inputs may be any that keep to these rules, and one draw needn't show every extreme that they name: `doc_lengths`: the rollout lengths sum to 8192; the first rollout is the longest, exactly 4096 tokens.
All inputs are finite; a program needn't handle non-finite values.
Results may differ from the reference program's by a relative error of at most 0.0045.
Values may be sent and summed in bfloat16 or wider, within the bound.
A program may use at most 64 MiB of HBM per device.

```python
import jax
import jax.numpy as jnp
from jax import lax

QH = 64
KVH = 4
HD = 128
NDOCS = 16
TOKENS = 8192
MOST = 4096


def draw_queries(key, part):
    key = jax.random.fold_in(key, 11)
    base = jnp.clip(jax.random.normal(key, (2, TOKENS, QH * HD), jnp.float32), -4.0, 4.0)
    return base.astype(jnp.bfloat16)


def draw_keys(key, part):
    key = jax.random.fold_in(key, 23)
    base = jnp.clip(jax.random.normal(key, (2, TOKENS, KVH * HD), jnp.float32), -4.0, 4.0)
    return base.astype(jnp.bfloat16)


def draw_doc_lengths(key, part):
    key = jax.random.fold_in(key, 37)
    remain = TOKENS - MOST
    picked = jax.random.permutation(key, remain - 1)[:NDOCS - 2] + 1
    cuts = jnp.sort(picked.astype(jnp.int32))
    edges = jnp.concatenate([jnp.zeros((1,), jnp.int32), cuts, jnp.full((1,), remain, jnp.int32)])
    rest = edges[1:] - edges[:-1]
    return jnp.concatenate([jnp.full((1,), MOST, jnp.int32), rest]).astype(jnp.int32)


def steps_of(own_key, extent, pieces, smallest, top_value):
    level, own = 1.0, jax.random.fold_in(own_key, 6)
    for axis_at, blocks in pieces:
        draws = jnp.exp(jax.random.uniform(jax.random.fold_in(own, axis_at), (blocks,), jnp.float32, smallest / len(pieces), top_value / len(pieces)))
        level = level * jnp.repeat(draws, extent[axis_at] // blocks).reshape([-1 if axis == axis_at else 1 for axis in range(len(extent))])
    return level


def noise(stream_key, dims, deviation, limit, shards=(), kind=jnp.bfloat16):
    gain = steps_of(stream_key, dims, shards, -0.22, 0.18) if shards else 1.0
    result = jax.random.normal(stream_key, dims, jnp.float32) * deviation * gain
    return jnp.minimum(jnp.maximum(result, -limit), limit).astype(kind)


def setup_inputs(seed: int = 0) -> dict:
    splits = jax.random.split(jax.random.key(seed), 5)
    return {
        "queries": draw_queries(jax.random.fold_in(splits[4], 71), 0),
        "keys": draw_keys(jax.random.fold_in(splits[4], 71), 0),
        "values": noise(splits[2], (2, TOKENS, KVH * HD), 1.0, 6.0, ((1, 64),)),
        "doc_lengths": draw_doc_lengths(jax.random.fold_in(splits[4], 71), 0),
    }


def reference(queries, keys, values, doc_lengths):
    tokens = queries.shape[1]
    group_size = QH // KVH
    scale = HD ** -0.5
    doc_ends = jnp.cumsum(doc_lengths)
    positions = jnp.arange(tokens, dtype=jnp.int32)
    segment = jnp.sum((positions[:, None] >= doc_ends[None, :]).astype(jnp.int32), axis=1)
    visible = (segment[:, None] == segment[None, :]) & (positions[:, None] >= positions[None, :])
    query_heads = queries.reshape(2, tokens, QH, HD).transpose(0, 2, 1, 3)
    key_heads = keys.reshape(2, tokens, KVH, HD).transpose(0, 2, 1, 3)
    value_heads = values.reshape(2, tokens, KVH, HD).transpose(0, 2, 1, 3)

    def one_head(index):
        model = index // QH
        head = index % QH
        query_one = query_heads[model, head]
        key_one = key_heads[model, head // group_size]
        value_one = value_heads[model, head // group_size]
        scores = jnp.dot(query_one, key_one.T, preferred_element_type=jnp.float32) * scale
        scores = jnp.where(visible, scores, jnp.float32(-1e30))
        row_max = jnp.max(scores, axis=1)
        weights = jnp.where(visible, jnp.exp(scores - row_max[:, None]), jnp.float32(0.0))
        totals = jnp.sum(weights, axis=1)
        summed = jnp.dot(weights.astype(jnp.bfloat16), value_one, preferred_element_type=jnp.float32)
        return (summed / totals[:, None]).astype(jnp.bfloat16), row_max + jnp.log(totals)

    outputs, log_norm = lax.map(one_head, jnp.arange(2 * QH, dtype=jnp.int32))
    attended = outputs.reshape(2, QH, tokens, HD).transpose(0, 2, 1, 3).reshape(2, tokens, QH * HD)
    log_norm = log_norm.reshape(2, QH, tokens)
    lse_gap = jnp.sum(log_norm[0] - log_norm[1], axis=0) / QH
    return attended, lse_gap
```

```python
import functools

import jax
import jax.numpy as jnp
from jax import lax
from jax.experimental import pallas as pl
from jax.experimental.pallas import tpu as pltpu
from jax.sharding import PartitionSpec as P

QH = 64
KVH = 4
HD = 128
TOKENS = 8192
MOST = 4096
NDOCS = 16

ROWS_Y = 8
HALF_Y = 4
Z_LO = 4
CORES = 2
Z_HI = 2
TP = 8
BLOCK = 128
ROW_KEYS = Z_LO * CORES * BLOCK
HEADS = QH // TP
TILE = 256

LOG2E = 1.4426950408889634
LN2 = 0.6931471805599453
LOG2_SCALE = HD**-0.5 * LOG2E
MASKED = -1e30
MESH = pl.DeviceIdType.MESH


def kernel(
    q_hbm, k_hbm, v_hbm, doc_ref, out_hbm, lse_ref,
    kv, q_vm, o_vm, acc, peak, total, first, gaps,
    load_sem, out_sem, y_send, y_recv, z_send, z_recv, f_send, f_recv, s_send, s_recv, g_send, g_recv,
):
    ctx = lax.axis_index("ctx")
    tp = lax.axis_index("tp")
    y = ctx // (Z_LO * CORES)
    z_lo = (ctx // CORES) % Z_LO
    core = ctx % CORES
    x = tp // Z_HI
    z = (tp % Z_HI) * Z_LO + z_lo
    half = y // HALF_Y
    row = y % HALF_Y
    steps = 2 * (row + 1)

    def at_z(where):
        where = (where + 2 * Z_HI * Z_LO) % (Z_HI * Z_LO)
        return (y * (Z_LO * CORES) + (where % Z_LO) * CORES + core, x * Z_HI + where // Z_LO)

    def at_row(where):
        return ((half * HALF_Y + where) * (Z_LO * CORES) + z_lo * CORES + core, tp)

    above, below = at_z(z + 1), at_z(z - 1)
    sibling = (ctx + 1 - 2 * core, tp)
    z_next, z_prev, z_far = (z_lo + 1) % Z_LO, (z_lo + 3) % Z_LO, (z_lo + 2) % Z_LO

    head = pl.ds(pl.multiple_of(x * HD, HD), HD)
    loads = []
    for m in range(2):
        loads.append(pltpu.make_async_copy(k_hbm.at[m, :, head], kv.at[m, row, 0, z_lo, core], load_sem.at[m, 0]))
        loads.append(pltpu.make_async_copy(v_hbm.at[m, :, head], kv.at[m, row, 1, z_lo, core], load_sem.at[m, 1]))
    for m in range(2):
        loads.append(pltpu.make_async_copy(q_hbm.at[m], q_vm.at[m], load_sem.at[m, 2]))
    for load in loads:
        load.start()

    barrier = pltpu.get_barrier_semaphore()

    def greet(device):
        pl.semaphore_signal(barrier, inc=1, device_id=device, device_id_type=MESH)

    greet(above)
    greet(below)
    greet(sibling)
    for other in range(1, HALF_Y):
        greet(at_row((row + other) % HALF_Y))
    for other in range(1, TP):
        greet((ctx, (tp + other) % TP))

    position = ctx * BLOCK + lax.broadcasted_iota(jnp.int32, (BLOCK, 128), 0)
    begin = jnp.zeros((BLOCK, 128), jnp.int32)
    end = jnp.int32(0)
    for doc in range(NDOCS):
        end = end + doc_ref[doc]
        begin = jnp.where(position >= end, end, begin)
    first[...] = begin

    for load in loads[:4]:
        load.wait()
    pl.semaphore_wait(barrier, 3 + (HALF_Y - 1) + (TP - 1))

    def step_of(step):
        return step % 2, row - step // 2

    def remote(src, dst, send, recv, device):
        return pltpu.make_async_remote_copy(
            src_ref=src, dst_ref=dst, send_sem=send, recv_sem=recv, device_id=device, device_id_type=MESH
        )

    def up_copy(m, other):
        mine = kv.at[m, row, :, z_lo, core]
        return remote(mine, mine, y_send.at[m, other], y_recv.at[m, row], at_row(other))

    def from_row(m, r):
        block = kv.at[m, r, :, z_lo, core]
        return remote(block, block, y_send.at[m, 0], y_recv.at[m, r], at_row(r))

    def z_copy(m, r, way):
        block = kv.at[m, r, :, z_lo, core]
        return remote(block, block, z_send.at[m, r, way], z_recv.at[m, r, way], below if way else above)

    def z_arrival(m, r, way):
        block = kv.at[m, r, :, z_next if way else z_prev, core]
        return remote(block, block, z_send.at[m, r, way], z_recv.at[m, r, way], above if way else below)

    def far_copy(m, r, way):
        block = kv.at[m, r, way, z_next if way else z_prev, core]
        return remote(block, block, f_send.at[m, r, way], f_recv.at[m, r, way], below if way else above)

    def far_arrival(m, r, way):
        block = kv.at[m, r, way, z_far, core]
        return remote(block, block, f_send.at[m, r, way], f_recv.at[m, r, way], above if way else below)

    columns = (z_lo, z_prev, z_next, z_far)

    def sib_copy(m, r, kind):
        block = kv.at[m, r, :, columns[kind], core]
        return remote(block, block, s_send.at[m, r, kind], s_recv.at[m, r, kind], sibling)

    def sib_arrival(m, r, kind):
        block = kv.at[m, r, :, columns[kind], 1 - core]
        return remote(block, block, s_send.at[m, r, kind], s_recv.at[m, r, kind], sibling)

    def spread(step, own):
        m, r = step_of(step)
        if not own:
            from_row(m, r).wait_recv()
        z_copy(m, r, 0).start()
        z_copy(m, r, 1).start()
        sib_copy(m, r, 0).start()

    def relay(step):
        m, r = step_of(step)
        for way in range(2):
            z_arrival(m, r, way).wait_recv()
            far_copy(m, r, way).start()
            sib_copy(m, r, 1 + way).start()

    def finish(step):
        m, r = step_of(step)
        for way in range(2):
            far_arrival(m, r, way).wait_recv()
        sib_copy(m, r, 3).start()

    def gather_done(step):
        m, r = step_of(step)
        for kind in range(4):
            sib_arrival(m, r, kind).wait_recv()

    def attend(step, causal):
        m, r = step_of(step)
        key_base = (half * HALF_Y + r) * ROW_KEYS
        keys = kv[m, r, 0].reshape(ROW_KEYS, HD)
        values = kv[m, r, 1].reshape(ROW_KEYS, HD)
        values = jnp.concatenate([values, jnp.ones((ROW_KEYS, 128), jnp.bfloat16)], axis=1)
        low = first[...] - key_base
        low = jnp.concatenate([low] * (TILE // BLOCK), axis=0)[:, :1]
        key_at = lax.broadcasted_iota(jnp.int32, (TILE, ROW_KEYS), 1)
        for tile in range(HEADS * BLOCK // TILE):
            rows = pl.ds(tile * TILE, TILE)
            heads = range(tile * (TILE // BLOCK), (tile + 1) * (TILE // BLOCK))
            q = jnp.concatenate([q_vm[m, :, pl.ds(h * HD, HD)] for h in heads], axis=0)
            scores = lax.dot_general(q, keys, (((1,), (1,)), ((), ())), preferred_element_type=jnp.float32)
            visible = key_at >= low
            if causal:
                query_at = lax.broadcasted_iota(jnp.int32, (TILE, ROW_KEYS), 0) % BLOCK
                query_at = query_at + (z_lo * CORES + core) * BLOCK
                visible = visible & (key_at <= query_at)
            scores = jnp.where(visible, scores, MASKED)
            here = jnp.max(scores, axis=1, keepdims=True) * LOG2_SCALE
            if causal:
                top = jnp.broadcast_to(here, (TILE, 128))
            else:
                old = peak[m, rows, :]
                top = jnp.maximum(old, here)
                factor = jnp.exp2(old - top)
            weights = jnp.exp2(scores * LOG2_SCALE - top[:, :1]).astype(jnp.bfloat16)
            both = jnp.dot(weights, values, preferred_element_type=jnp.float32)
            if causal:
                acc[m, rows, :] = both[:, :HD]
                total[m, rows, :] = both[:, HD:]
            else:
                acc[m, rows, :] = acc[m, rows, :] * factor + both[:, :HD]
                total[m, rows, :] = total[m, rows, :] * factor + both[:, HD:]
            peak[m, rows, :] = top

    def when_live(step, act):
        @pl.when(step < steps)
        def _():
            act(step)

    spread(0, True)
    for other in range(1, HALF_Y):
        @pl.when(other > row)
        def _():
            up_copy(0, other).start()
    spread(1, True)
    for other in range(1, HALF_Y):
        @pl.when(other > row)
        def _():
            up_copy(1, other).start()
    relay(0)
    when_live(2, lambda step: spread(step, False))
    relay(1)
    finish(0)
    for load in loads[4:]:
        load.wait()

    def slot(step, causal):
        gather_done(step)
        when_live(step + 1, finish)
        when_live(step + 2, relay)
        when_live(step + 3, lambda later: spread(later, False))
        attend(step, causal)
        return 0

    lax.fori_loop(0, 2, lambda step, _: slot(step, True), 0)
    lax.fori_loop(2, steps, lambda step, _: slot(step, False), 0)

    gap = jnp.zeros((BLOCK, 128), jnp.float32)
    for h in range(HEADS):
        rows = pl.ds(h * BLOCK, BLOCK)
        gap = gap + ((peak[0, rows, :] - peak[1, rows, :]) * LN2 + (jnp.log(total[0, rows, :]) - jnp.log(total[1, rows, :])))
    gaps[tp] = gap.T[:8, :]

    def gap_copy(other):
        return remote(gaps.at[tp], gaps.at[tp], g_send.at[other], g_recv.at[tp], (ctx, (tp + other) % TP))

    def gap_arrival(other):
        peer = (tp + other) % TP
        return remote(gaps.at[peer], gaps.at[peer], g_send.at[other], g_recv.at[peer], (ctx, peer))

    for other in range(1, TP):
        gap_copy(other).start()

    stores = []
    for m in range(2):
        for h in range(HEADS):
            rows = pl.ds(h * BLOCK, BLOCK)
            o_vm[m, :, pl.ds(h * HD, HD)] = (acc[m, rows, :] / total[m, rows, :]).astype(jnp.bfloat16)
        stores.append(pltpu.make_async_copy(o_vm.at[m], out_hbm.at[m], out_sem.at[m]))
        stores[m].start()

    def wait_sends(step, _):
        m, r = step_of(step)
        for way in range(2):
            z_copy(m, r, way).wait_send()
            far_copy(m, r, way).wait_send()
        for kind in range(4):
            sib_copy(m, r, kind).wait_send()
        return 0

    lax.fori_loop(0, steps, wait_sends, 0)
    for m in range(2):
        for other in range(1, HALF_Y):
            @pl.when(other > row)
            def _():
                up_copy(m, other).wait_send()

    for other in range(1, TP):
        gap_arrival(other).wait_recv()
    whole = gaps[0]
    for peer in range(1, TP):
        whole = whole + gaps[peer]
    lse_ref[...] = whole[:1, :] * (1.0 / QH)
    for other in range(1, TP):
        gap_copy(other).wait_send()
    for store in stores:
        store.wait()


def per_device(queries, keys, values, doc_lengths):
    dma = pltpu.SemaphoreType.DMA
    attended, gap = pl.pallas_call(
        kernel,
        out_shape=[
            jax.ShapeDtypeStruct((2, BLOCK, HEADS * HD), jnp.bfloat16),
            jax.ShapeDtypeStruct((1, BLOCK), jnp.float32),
        ],
        in_specs=[pl.BlockSpec(memory_space=pl.ANY)] * 3 + [pl.BlockSpec(memory_space=pltpu.SMEM)],
        out_specs=[pl.BlockSpec(memory_space=pl.ANY), pl.BlockSpec(memory_space=pltpu.VMEM)],
        scratch_shapes=[
            pltpu.VMEM((2, HALF_Y, 2, Z_LO, CORES, BLOCK, HD), jnp.bfloat16),
            pltpu.VMEM((2, BLOCK, HEADS * HD), jnp.bfloat16),
            pltpu.VMEM((2, BLOCK, HEADS * HD), jnp.bfloat16),
            pltpu.VMEM((2, HEADS * BLOCK, HD), jnp.float32),
            pltpu.VMEM((2, HEADS * BLOCK, 128), jnp.float32),
            pltpu.VMEM((2, HEADS * BLOCK, 128), jnp.float32),
            pltpu.VMEM((BLOCK, 128), jnp.int32),
            pltpu.VMEM((TP, 8, 128), jnp.float32),
            dma((2, 3)),
            dma((2,)),
            dma((2, HALF_Y)),
            dma((2, HALF_Y)),
            dma((2, HALF_Y, 2)),
            dma((2, HALF_Y, 2)),
            dma((2, HALF_Y, 2)),
            dma((2, HALF_Y, 2)),
            dma((2, HALF_Y, 4)),
            dma((2, HALF_Y, 4)),
            dma((TP,)),
            dma((TP,)),
        ],
        compiler_params=pltpu.CompilerParams(
            collective_id=0, has_side_effects=True, vmem_limit_bytes=48 * 2**20
        ),
        name="packed_attention",
    )(queries, keys, values, doc_lengths)
    return attended, gap.reshape(BLOCK)


def solution(mesh):
    in_specs = (P(None, "ctx", "tp"), P(None, "ctx", None), P(None, "ctx", None), P())
    out_specs = (P(None, "ctx", "tp"), P("ctx"))
    return jax.shard_map(
        per_device, mesh=mesh, in_specs=in_specs, out_specs=out_specs, check_vma=False
    )
```

```python
import functools

import jax
import jax.numpy as jnp
from jax import lax
from jax.experimental import pallas as pl
from jax.experimental.pallas import tpu as pltpu
from jax.sharding import PartitionSpec as P

QH = 64
KVH = 4
HD = 128
TOKENS = 8192
MOST = 4096
NDOCS = 16

ROWS_Y = 8
HALF_Y = 4
Z_LO = 4
CORES = 2
Z_HI = 2
TP = 8
BLOCK = 128
ROW_KEYS = Z_LO * CORES * BLOCK
HEADS = QH // TP
TILE = 256

LOG2E = 1.4426950408889634
LN2 = 0.6931471805599453
LOG2_SCALE = HD**-0.5 * LOG2E
MASKED = -1e30
EMPTY = -1e35
MESH = pl.DeviceIdType.MESH


AHEAD = {
    0: (("relay", 1),),
    1: (("finish", 1), ("spread", 4)),
    2: (("relay", 2), ("spread", 5)),
    3: (("finish", 2),),
    4: (("relay", 3), ("spread", 6)),
    5: (("finish", 3), ("spread", 7)),
    7: (("relay", 4), ("finish", 4)),
    9: (("relay", 5), ("finish", 5)),
    11: (("relay", 6), ("finish", 6)),
    13: (("relay", 7), ("finish", 7)),
}


def kernel(
    q_hbm, k_hbm, v_hbm, doc_ref, out_hbm, lse_ref,
    kv, q_vm, o_vm, acc, peak, total, bias, eye, scores_0, scores_1, weights_0, weights_1, factor_0, factor_1, gaps,
    load_sem, out_sem, y_send, y_recv, z_send, z_recv, f_send, f_recv, s_send, s_recv, u_send, u_recv, g_send, g_recv,
):
    ctx = lax.axis_index("ctx")
    tp = lax.axis_index("tp")
    y = ctx // (Z_LO * CORES)
    z_lo = (ctx // CORES) % Z_LO
    core = ctx % CORES
    x = tp // Z_HI
    z = (tp % Z_HI) * Z_LO + z_lo
    half = y // HALF_Y
    row = y % HALF_Y
    steps = 2 * (row + 1)

    def at_z(where):
        where = (where + 2 * Z_HI * Z_LO) % (Z_HI * Z_LO)
        return (y * (Z_LO * CORES) + (where % Z_LO) * CORES + core, x * Z_HI + where // Z_LO)

    def at_row(where):
        return ((half * HALF_Y + where) * (Z_LO * CORES) + z_lo * CORES + core, tp)

    above, below = at_z(z + 1), at_z(z - 1)
    sibling = (ctx + 1 - 2 * core, tp)
    z_next, z_prev, z_far = (z_lo + 1) % Z_LO, (z_lo + 3) % Z_LO, (z_lo + 2) % Z_LO

    head = pl.ds(pl.multiple_of(x * HD, HD), HD)
    loads = []
    for m in range(2):
        loads.append(pltpu.make_async_copy(k_hbm.at[m, :, head], kv.at[m, row, 0, z_lo, core], load_sem.at[m, 0]))
        loads.append(pltpu.make_async_copy(v_hbm.at[m, :, head], kv.at[m, row, 1, z_lo, core], load_sem.at[m, 1]))
    for m in range(2):
        loads.append(pltpu.make_async_copy(q_hbm.at[m], q_vm.at[m], load_sem.at[m, 2]))
    for load in loads:
        load.start()

    barrier = pltpu.get_barrier_semaphore()

    def greet(device):
        pl.semaphore_signal(barrier, inc=1, device_id=device, device_id_type=MESH)

    greet(above)
    greet(below)
    greet(at_z(z + 2))
    greet(at_z(z - 2))
    greet(sibling)
    for other in range(1, HALF_Y):
        greet(at_row((row + other) % HALF_Y))
    for other in range(1, TP):
        greet((ctx, (tp + other) % TP))

    position = ctx * BLOCK + lax.broadcasted_iota(jnp.int32, (8, BLOCK), 1)
    begin = jnp.zeros((8, BLOCK), jnp.int32)
    end = jnp.int32(0)
    for doc in range(NDOCS):
        end = end + doc_ref[doc]
        begin = jnp.where(position >= end, end, begin)

    acc[...] = jnp.zeros_like(acc)
    total[...] = jnp.zeros_like(total)
    peak[...] = jnp.full_like(peak, MASKED)
    scores_1[...] = jnp.full_like(scores_1, EMPTY)
    for ref in (weights_0, weights_1):
        ref[...] = jnp.zeros_like(ref)
    for ref in (factor_0, factor_1):
        ref[...] = jnp.ones_like(ref)
    eye[...] = (
        lax.broadcasted_iota(jnp.int32, (BLOCK, BLOCK), 0) == lax.broadcasted_iota(jnp.int32, (BLOCK, BLOCK), 1)
    ).astype(jnp.bfloat16)

    for load in loads[:4]:
        load.wait()
    pl.semaphore_wait(barrier, 5 + (HALF_Y - 1) + (TP - 1))

    def step_of(step):
        return step % 2, row - step // 2

    def remote(src, dst, send, recv, device):
        return pltpu.make_async_remote_copy(
            src_ref=src, dst_ref=dst, send_sem=send, recv_sem=recv, device_id=device, device_id_type=MESH
        )

    def up_copy(m, other):
        mine = kv.at[m, row, :, z_lo, core]
        return remote(mine, mine, y_send.at[m, other], y_recv.at[m, row], at_row(other))

    def from_row(m, r):
        block = kv.at[m, r, :, z_lo, core]
        return remote(block, block, y_send.at[m, 0], y_recv.at[m, r], at_row(r))

    def z_copy(m, r, way):
        block = kv.at[m, r, :, z_lo, core]
        return remote(block, block, z_send.at[m, r, way], z_recv.at[m, r, way], below if way else above)

    def z_arrival(m, r, way):
        block = kv.at[m, r, :, z_next if way else z_prev, core]
        return remote(block, block, z_send.at[m, r, way], z_recv.at[m, r, way], above if way else below)

    def far_copy(m, r, way):
        block = kv.at[m, r, way, z_lo, core]
        return remote(block, block, f_send.at[m, r, way], f_recv.at[m, r, way], at_z(z - 2 if way else z + 2))

    def far_arrival(m, r, way):
        block = kv.at[m, r, way, z_far, core]
        return remote(block, block, f_send.at[m, r, way], f_recv.at[m, r, way], at_z(z + 2 if way else z - 2))

    def far_up(m):
        block = kv.at[m, row, :, z_far, core]
        return remote(block, block, u_send.at[m], u_recv.at[m, row], at_row(HALF_Y - 1))

    def far_from_row(m, r):
        block = kv.at[m, r, :, z_far, core]
        return remote(block, block, u_send.at[m], u_recv.at[m, r], at_row(r))

    top_row = row == HALF_Y - 1
    sends_far_up = row < HALF_Y - 2

    columns = (z_lo, z_prev, z_next, z_far)

    def sib_copy(m, r, kind):
        block = kv.at[m, r, :, columns[kind], core]
        return remote(block, block, s_send.at[m, r, kind], s_recv.at[m, r, kind], sibling)

    def sib_arrival(m, r, kind):
        block = kv.at[m, r, :, columns[kind], 1 - core]
        return remote(block, block, s_send.at[m, r, kind], s_recv.at[m, r, kind], sibling)

    def pass_on(m, r):
        for way in range(2):
            z_copy(m, r, way).start()
        sib_copy(m, r, 0).start()

    def far_by_z(step):
        return jnp.logical_not(top_row & (step >= 4))

    def spread(step):
        m, r = step_of(step)
        from_row(m, r).wait_recv()
        pass_on(m, r)

        @pl.when(far_by_z(step))
        def _():
            for way in range(2):
                far_copy(m, r, way).start()

    def relay(step):
        m, r = step_of(step)
        for way in range(2):
            z_arrival(m, r, way).wait_recv()
            sib_copy(m, r, 1 + way).start()

    def finish(step):
        m, r = step_of(step)

        @pl.when(far_by_z(step))
        def _():
            for way in range(2):
                far_arrival(m, r, way).wait_recv()

        @pl.when(jnp.logical_not(far_by_z(step)))
        def _():
            far_from_row(m, r).wait_recv()

        sib_copy(m, r, 3).start()

        @pl.when(sends_far_up & (step < 2))
        def _():
            far_up(m).start()

    def gather_done(step):
        m, r = step_of(step)
        for kind in range(4):
            sib_arrival(m, r, kind).wait_recv()

    pairs = HEADS * BLOCK // TILE // 2
    tile_heads = TILE // BLOCK
    scores, weights, factors = (scores_0, scores_1), (weights_0, weights_1), (factor_0, factor_1)

    def place(tile):
        tile = jnp.maximum(tile, 0)
        m, r = step_of(tile // (2 * pairs))
        return m, r, tile % (2 * pairs)

    def score(tile, slot):
        m, r, at = place(tile)
        heads = [
            q_vm[m, :, pl.ds(pl.multiple_of((at * tile_heads + h) * HD, HD), HD)] for h in range(tile_heads)
        ]
        q = jnp.concatenate([jnp.concatenate([h, eye[...]], axis=1) for h in heads], axis=0)
        keys = jnp.concatenate([kv[m, r, 0].reshape(ROW_KEYS, HD), bias[r]], axis=1)
        scores[slot][...] = lax.dot_general(q, keys, (((1,), (1,)), ((), ())), preferred_element_type=jnp.float32)

    def weigh(tile, slot):
        m, r, at = place(tile)
        rows = pl.ds(pl.multiple_of(at * TILE, TILE), TILE)
        here = scores[slot][...]
        old = peak[m, rows, :]
        new = jnp.maximum(old, jnp.max(here, axis=1, keepdims=True) * LOG2_SCALE)
        factors[slot][...] = jnp.exp2(old - new)
        peak[m, rows, :] = new
        weights[slot][...] = jnp.exp2(here * LOG2_SCALE - new[:, :1]).astype(jnp.bfloat16)

    def gather(tile, slot):
        m, r, at = place(tile)
        rows = pl.ds(pl.multiple_of(at * TILE, TILE), TILE)
        values = jnp.concatenate([kv[m, r, 1].reshape(ROW_KEYS, HD), jnp.ones((ROW_KEYS, 128), jnp.bfloat16)], axis=1)
        both = jnp.dot(weights[slot][...], values, preferred_element_type=jnp.float32)
        acc[m, rows, :] = acc[m, rows, :] * factors[slot][...] + both[:, :HD]
        total[m, rows, :] = total[m, rows, :] * factors[slot][...] + both[:, HD:]

    def mask_row(r, _):
        key_at = (half * HALF_Y + r) * ROW_KEYS + lax.broadcasted_iota(jnp.int32, (ROW_KEYS, BLOCK), 0)
        visible = (key_at >= begin[:1, :]) & (key_at <= position[:1, :])
        bias[r] = jnp.where(visible, 0.0, MASKED).astype(jnp.bfloat16)
        return 0

    def when_live(step, act):
        @pl.when(step < steps)
        def _():
            act(step)

    def up(other):
        @pl.when(other < HALF_Y)
        def _():
            for m in range(2):
                up_copy(m, other).start()

    for m in range(2):
        pass_on(m, row)
        for way in range(2):
            far_copy(m, row, way).start()
    up(row + 1)
    lax.fori_loop(0, row + 1, mask_row, 0)
    relay(0)
    for other in (3, 2):
        @pl.when(other > row + 1)
        def _():
            up(other)
    when_live(2, spread)
    finish(0)
    when_live(3, spread)
    for load in loads[4:]:
        load.wait()

    def pair(at, _):
        for here, acts in AHEAD.items():
            @pl.when(at == here)
            def _():
                for act, step in acts:
                    when_live(step, {"spread": spread, "relay": relay, "finish": finish}[act])

        @pl.when(at % pairs == 0)
        def _():
            gather_done(at // pairs)

        tile = 2 * at
        score(tile, 0)
        weigh(tile - 1, 1)
        gather(tile - 2, 0)
        score(tile + 1, 1)
        weigh(tile, 0)
        gather(tile - 1, 1)
        return 0

    lax.fori_loop(0, pairs * steps, pair, 0)
    tiles = 2 * pairs * steps
    weigh(tiles - 1, 1)
    gather(tiles - 2, 0)
    gather(tiles - 1, 1)

    gap = jnp.zeros((BLOCK, 128), jnp.float32)
    for h in range(HEADS):
        rows = pl.ds(h * BLOCK, BLOCK)
        gap = gap + ((peak[0, rows, :] - peak[1, rows, :]) * LN2 + (jnp.log(total[0, rows, :]) - jnp.log(total[1, rows, :])))
    gaps[tp] = gap.T[:8, :]

    def gap_copy(other):
        return remote(gaps.at[tp], gaps.at[tp], g_send.at[other], g_recv.at[tp], (ctx, (tp + other) % TP))

    def gap_arrival(other):
        peer = (tp + other) % TP
        return remote(gaps.at[peer], gaps.at[peer], g_send.at[other], g_recv.at[peer], (ctx, peer))

    for other in range(1, TP):
        gap_copy(other).start()

    stores = []
    for m in range(2):
        for h in range(HEADS):
            rows = pl.ds(h * BLOCK, BLOCK)
            o_vm[m, :, pl.ds(h * HD, HD)] = (acc[m, rows, :] / total[m, rows, :]).astype(jnp.bfloat16)
        stores.append(pltpu.make_async_copy(o_vm.at[m], out_hbm.at[m], out_sem.at[m]))
        stores[m].start()

    def wait_sends(step, _):
        m, r = step_of(step)
        for way in range(2):
            z_copy(m, r, way).wait_send()

        @pl.when(far_by_z(step))
        def _():
            for way in range(2):
                far_copy(m, r, way).wait_send()

        for kind in range(4):
            sib_copy(m, r, kind).wait_send()
        return 0

    lax.fori_loop(0, steps, wait_sends, 0)
    for m in range(2):
        for other in range(1, HALF_Y):
            @pl.when(other > row)
            def _():
                up_copy(m, other).wait_send()

        @pl.when(sends_far_up)
        def _():
            far_up(m).wait_send()

    for other in range(1, TP):
        gap_arrival(other).wait_recv()
    whole = gaps[0]
    for peer in range(1, TP):
        whole = whole + gaps[peer]
    lse_ref[...] = whole[:1, :] * (1.0 / QH)
    for other in range(1, TP):
        gap_copy(other).wait_send()
    for store in stores:
        store.wait()


def per_device(queries, keys, values, doc_lengths):
    dma = pltpu.SemaphoreType.DMA
    attended, gap = pl.pallas_call(
        kernel,
        out_shape=[
            jax.ShapeDtypeStruct((2, BLOCK, HEADS * HD), jnp.bfloat16),
            jax.ShapeDtypeStruct((1, BLOCK), jnp.float32),
        ],
        in_specs=[pl.BlockSpec(memory_space=pl.ANY)] * 3 + [pl.BlockSpec(memory_space=pltpu.SMEM)],
        out_specs=[pl.BlockSpec(memory_space=pl.ANY), pl.BlockSpec(memory_space=pltpu.VMEM)],
        scratch_shapes=[
            pltpu.VMEM((2, HALF_Y, 2, Z_LO, CORES, BLOCK, HD), jnp.bfloat16),
            pltpu.VMEM((2, BLOCK, HEADS * HD), jnp.bfloat16),
            pltpu.VMEM((2, BLOCK, HEADS * HD), jnp.bfloat16),
            pltpu.VMEM((2, HEADS * BLOCK, HD), jnp.float32),
            pltpu.VMEM((2, HEADS * BLOCK, 128), jnp.float32),
            pltpu.VMEM((2, HEADS * BLOCK, 128), jnp.float32),
            pltpu.VMEM((HALF_Y, ROW_KEYS, BLOCK), jnp.bfloat16),
            pltpu.VMEM((BLOCK, BLOCK), jnp.bfloat16),
            pltpu.VMEM((TILE, ROW_KEYS), jnp.float32),
            pltpu.VMEM((TILE, ROW_KEYS), jnp.float32),
            pltpu.VMEM((TILE, ROW_KEYS), jnp.bfloat16),
            pltpu.VMEM((TILE, ROW_KEYS), jnp.bfloat16),
            pltpu.VMEM((TILE, 128), jnp.float32),
            pltpu.VMEM((TILE, 128), jnp.float32),
            pltpu.VMEM((TP, 8, 128), jnp.float32),
            dma((2, 3)),
            dma((2,)),
            dma((2, HALF_Y)),
            dma((2, HALF_Y)),
            dma((2, HALF_Y, 2)),
            dma((2, HALF_Y, 2)),
            dma((2, HALF_Y, 2)),
            dma((2, HALF_Y, 2)),
            dma((2, HALF_Y, 4)),
            dma((2, HALF_Y, 4)),
            dma((2,)),
            dma((2, HALF_Y)),
            dma((TP,)),
            dma((TP,)),
        ],
        compiler_params=pltpu.CompilerParams(
            collective_id=0, has_side_effects=True, vmem_limit_bytes=60 * 2**20
        ),
        name="packed_attention",
    )(queries, keys, values, doc_lengths)
    return attended, gap.reshape(BLOCK)


def solution(mesh):
    in_specs = (P(None, "ctx", "tp"), P(None, "ctx", None), P(None, "ctx", None), P())
    out_specs = (P(None, "ctx", "tp"), P("ctx"))
    return jax.shard_map(
        per_device, mesh=mesh, in_specs=in_specs, out_specs=out_specs, check_vma=False
    )
```

```python
import functools

import jax
import jax.numpy as jnp
from jax import lax
from jax.experimental import pallas as pl
from jax.experimental.pallas import tpu as pltpu
from jax.sharding import PartitionSpec as P

QH = 64
KVH = 4
HD = 128
TOKENS = 8192
MOST = 4096
NDOCS = 16

ROWS_Y = 8
HALF_Y = 4
Z_LO = 4
CORES = 2
Z_HI = 2
TP = 8
BLOCK = 128
ROW_KEYS = Z_LO * CORES * BLOCK
HEADS = QH // TP
TILE = 256

LOG2E = 1.4426950408889634
LN2 = 0.6931471805599453
LOG2_SCALE = HD**-0.5 * LOG2E
MASKED = -1e30
EMPTY = -1e35
MESH = pl.DeviceIdType.MESH


AHEAD_TOP = {
    0: (("relay", 1),),
    1: (("finish", 1), ("spread", 4),),
    2: (("relay", 2),),
    3: (("finish", 2), ("spread", 5),),
    4: (("relay", 3),),
    5: (("finish", 3),),
    6: (("spread", 6),),
    7: (("relay", 4), ("finish", 4), ("spread", 7),),
    9: (("relay", 5), ("finish", 5),),
    11: (("relay", 6), ("finish", 6),),
    13: (("relay", 7), ("finish", 7),),
}
AHEAD_LOW = {
    0: (("relay", 1),),
    1: (("finish", 1), ("spread", 4),),
    2: (("relay", 2), ("spread", 5),),
    3: (("finish", 2),),
    4: (("relay", 3),),
    5: (("finish", 3),),
    7: (("relay", 4), ("finish", 4),),
    9: (("relay", 5), ("finish", 5),),
    11: (("relay", 6), ("finish", 6),),
    13: (("relay", 7), ("finish", 7),),
}


def kernel(
    q_hbm, k_hbm, v_hbm, doc_ref, out_ref, lse_ref,
    kv, q_vm, acc, peak, total, bias, eye, scores_0, scores_1, weights_0, weights_1, factor_0, factor_1, gaps,
    load_sem, y_send, y_recv, z_send, z_recv, f_send, f_recv, s_send, s_recv, u_send, u_recv, g_send, g_recv,
):
    ctx = lax.axis_index("ctx")
    tp = lax.axis_index("tp")
    y = ctx // (Z_LO * CORES)
    z_lo = (ctx // CORES) % Z_LO
    core = ctx % CORES
    x = tp // Z_HI
    z = (tp % Z_HI) * Z_LO + z_lo
    half = y // HALF_Y
    row = y % HALF_Y
    steps = 2 * (row + 1)

    def at_z(where):
        where = (where + 2 * Z_HI * Z_LO) % (Z_HI * Z_LO)
        return (y * (Z_LO * CORES) + (where % Z_LO) * CORES + core, x * Z_HI + where // Z_LO)

    def at_row(where):
        return ((half * HALF_Y + where) * (Z_LO * CORES) + z_lo * CORES + core, tp)

    above, below = at_z(z + 1), at_z(z - 1)
    sibling = (ctx + 1 - 2 * core, tp)
    z_next, z_prev, z_far = (z_lo + 1) % Z_LO, (z_lo + 3) % Z_LO, (z_lo + 2) % Z_LO

    barrier = pltpu.get_barrier_semaphore()

    def greet(device):
        pl.semaphore_signal(barrier, inc=1, device_id=device, device_id_type=MESH)

    greet(above)
    greet(below)
    greet(at_z(z + 2))
    greet(at_z(z - 2))
    greet(sibling)
    for other in range(1, HALF_Y):
        greet(at_row((row + other) % HALF_Y))
    for other in range(1, TP):
        greet((ctx, (tp + other) % TP))

    head = pl.ds(pl.multiple_of(x * HD, HD), HD)
    loads = []
    for m in range(2):
        loads.append(pltpu.make_async_copy(k_hbm.at[m, :, head], kv.at[m, row, 0, z_lo, core], load_sem.at[m, 0]))
        loads.append(pltpu.make_async_copy(v_hbm.at[m, :, head], kv.at[m, row, 1, z_lo, core], load_sem.at[m, 1]))
    for m in range(2):
        loads.append(pltpu.make_async_copy(q_hbm.at[m], q_vm.at[m], load_sem.at[m, 2]))
    for load in loads:
        load.start()

    position = ctx * BLOCK + lax.broadcasted_iota(jnp.int32, (8, BLOCK), 1)
    begin = jnp.zeros((8, BLOCK), jnp.int32)
    end = jnp.int32(0)
    for doc in range(NDOCS):
        end = end + doc_ref[doc]
        begin = jnp.where(position >= end, end, begin)

    for load in loads[:4]:
        load.wait()
    pl.semaphore_wait(barrier, 5 + (HALF_Y - 1) + (TP - 1))

    def step_of(step):
        return step % 2, row - step // 2

    def remote(src, dst, send, recv, device):
        return pltpu.make_async_remote_copy(
            src_ref=src, dst_ref=dst, send_sem=send, recv_sem=recv, device_id=device, device_id_type=MESH
        )

    def up_copy(m, other):
        mine = kv.at[m, row, :, z_lo, core]
        return remote(mine, mine, y_send.at[m, other], y_recv.at[m, row], at_row(other))

    def up_relay(m, r):
        block = kv.at[m, r, :, z_lo, core]
        return remote(block, block, y_send.at[m, r], y_recv.at[m, r], at_row(HALF_Y - 1))

    def from_row(m, r):
        block = kv.at[m, r, :, z_lo, core]
        return remote(block, block, y_send.at[m, 0], y_recv.at[m, r], at_row(r))

    def z_copy(m, r, way):
        block = kv.at[m, r, :, z_lo, core]
        return remote(block, block, z_send.at[m, r, way], z_recv.at[m, r, way], below if way else above)

    def z_arrival(m, r, way):
        block = kv.at[m, r, :, z_next if way else z_prev, core]
        return remote(block, block, z_send.at[m, r, way], z_recv.at[m, r, way], above if way else below)

    def far_copy(m, r, way):
        block = kv.at[m, r, way, z_lo, core]
        return remote(block, block, f_send.at[m, r, way], f_recv.at[m, r, way], at_z(z - 2 if way else z + 2))

    def far_arrival(m, r, way):
        block = kv.at[m, r, way, z_far, core]
        return remote(block, block, f_send.at[m, r, way], f_recv.at[m, r, way], at_z(z + 2 if way else z - 2))

    def far_up(m):
        block = kv.at[m, row, :, z_far, core]
        return remote(block, block, u_send.at[m], u_recv.at[m, row], at_row(HALF_Y - 1))

    def far_from_row(m, r):
        block = kv.at[m, r, :, z_far, core]
        return remote(block, block, u_send.at[m], u_recv.at[m, r], at_row(r))

    top_row = row == HALF_Y - 1
    sends_far_up = row < HALF_Y - 2

    columns = (z_lo, z_prev, z_next, z_far)

    def sib_copy(m, r, kind):
        block = kv.at[m, r, :, columns[kind], core]
        return remote(block, block, s_send.at[m, r, kind], s_recv.at[m, r, kind], sibling)

    def sib_arrival(m, r, kind):
        block = kv.at[m, r, :, columns[kind], 1 - core]
        return remote(block, block, s_send.at[m, r, kind], s_recv.at[m, r, kind], sibling)

    def pass_on(m, r):
        for way in range(2):
            z_copy(m, r, way).start()
        sib_copy(m, r, 0).start()

    def far_by_z(step):
        return jnp.logical_not(top_row & (step >= 4))

    def spread(step):
        m, r = step_of(step)
        from_row(m, r).wait_recv()
        pass_on(m, r)

        @pl.when(row == HALF_Y - 2)
        def _():
            up_relay(m, r).start()

        @pl.when(far_by_z(step))
        def _():
            for way in range(2):
                far_copy(m, r, way).start()

    def relay(step):
        m, r = step_of(step)
        for way in range(2):
            z_arrival(m, r, way).wait_recv()
            sib_copy(m, r, 1 + way).start()

    def finish(step):
        m, r = step_of(step)

        @pl.when(far_by_z(step))
        def _():
            for way in range(2):
                far_arrival(m, r, way).wait_recv()

        @pl.when(jnp.logical_not(far_by_z(step)))
        def _():
            far_from_row(m, r).wait_recv()

        sib_copy(m, r, 3).start()

        @pl.when(sends_far_up & (step < 2))
        def _():
            far_up(m).start()

    def gather_done(step):
        m, r = step_of(step)
        for kind in range(4):
            sib_arrival(m, r, kind).wait_recv()

    pairs = HEADS * BLOCK // TILE // 2
    tile_heads = TILE // BLOCK
    scores, weights, factors = (scores_0, scores_1), (weights_0, weights_1), (factor_0, factor_1)

    def place(tile):
        tile = jnp.maximum(tile, 0)
        m, r = step_of(tile // (2 * pairs))
        return m, r, tile % (2 * pairs)

    def score(tile, slot):
        m, r, at = place(tile)
        heads = [
            q_vm[m, :, pl.ds(pl.multiple_of((at * tile_heads + h) * HD, HD), HD)] for h in range(tile_heads)
        ]
        q = jnp.concatenate([jnp.concatenate([h, eye[...]], axis=1) for h in heads], axis=0)
        keys = jnp.concatenate([kv[m, r, 0].reshape(ROW_KEYS, HD), bias[r]], axis=1)
        scores[slot][...] = lax.dot_general(q, keys, (((1,), (1,)), ((), ())), preferred_element_type=jnp.float32)

    def weigh(tile, slot):
        m, r, at = place(tile)
        rows = pl.ds(pl.multiple_of(at * TILE, TILE), TILE)
        here = scores[slot][...]
        old = peak[m, rows, :]
        new = jnp.maximum(old, jnp.max(here, axis=1, keepdims=True) * LOG2_SCALE)
        factors[slot][...] = jnp.exp2(old - new)
        peak[m, rows, :] = new
        weights[slot][...] = jnp.exp2(here * LOG2_SCALE - new[:, :1]).astype(jnp.bfloat16)

    def gather(tile, slot):
        m, r, at = place(tile)
        rows = pl.ds(pl.multiple_of(at * TILE, TILE), TILE)
        values = jnp.concatenate([kv[m, r, 1].reshape(ROW_KEYS, HD), jnp.ones((ROW_KEYS, 128), jnp.bfloat16)], axis=1)
        both = jnp.dot(weights[slot][...], values, preferred_element_type=jnp.float32)
        acc[m, rows, :] = acc[m, rows, :] * factors[slot][...] + both[:, :HD]
        total[m, rows, :] = total[m, rows, :] * factors[slot][...] + both[:, HD:]

    def mask_row(r, _):
        key_at = (half * HALF_Y + r) * ROW_KEYS + lax.broadcasted_iota(jnp.int32, (ROW_KEYS, BLOCK), 0)
        visible = (key_at >= begin[:1, :]) & (key_at <= position[:1, :])
        bias[r] = jnp.where(visible, 0.0, MASKED).astype(jnp.bfloat16)
        return 0

    def when_live(step, act):
        @pl.when(step < steps)
        def _():
            act(step)

    def up(m, other):
        @pl.when(other < HALF_Y)
        def _():
            up_copy(m, other).start()

    def open_row(m):
        pass_on(m, row)
        for way in range(2):
            far_copy(m, row, way).start()

    open_row(0)
    up(0, row + 1)
    up(1, row + 1)

    acc[...] = jnp.zeros_like(acc)
    total[...] = jnp.zeros_like(total)
    peak[...] = jnp.full_like(peak, MASKED)
    scores_1[...] = jnp.full_like(scores_1, EMPTY)
    for ref in (weights_0, weights_1):
        ref[...] = jnp.zeros_like(ref)
    for ref in (factor_0, factor_1):
        ref[...] = jnp.ones_like(ref)
    eye[...] = (
        lax.broadcasted_iota(jnp.int32, (BLOCK, BLOCK), 0) == lax.broadcasted_iota(jnp.int32, (BLOCK, BLOCK), 1)
    ).astype(jnp.bfloat16)

    for m in range(2):
        @pl.when(row == 0)
        def _():
            up(m, HALF_Y - 2)

    open_row(1)
    lax.fori_loop(0, row + 1, mask_row, 0)
    relay(0)
    when_live(2, spread)
    finish(0)
    when_live(3, spread)

    for load in loads[4:]:
        load.wait()

    def pair(at, _):
        for here, acts, mine in [(*item, top_row) for item in AHEAD_TOP.items()] + [
            (*item, jnp.logical_not(top_row)) for item in AHEAD_LOW.items()
        ]:
            @pl.when((at == here) & mine)
            def _():
                for act, step in acts:
                    when_live(step, {"spread": spread, "relay": relay, "finish": finish}[act])

        @pl.when(at % pairs == 0)
        def _():
            gather_done(at // pairs)

        tile = 2 * at
        score(tile, 0)
        weigh(tile - 1, 1)
        gather(tile - 2, 0)
        score(tile + 1, 1)
        weigh(tile, 0)
        gather(tile - 1, 1)
        return 0

    lax.fori_loop(0, pairs * steps, pair, 0)
    tiles = 2 * pairs * steps
    weigh(tiles - 1, 1)
    gather(tiles - 2, 0)
    gather(tiles - 1, 1)

    gap = jnp.zeros((BLOCK, 128), jnp.float32)
    for h in range(HEADS):
        rows = pl.ds(h * BLOCK, BLOCK)
        gap = gap + ((peak[0, rows, :] - peak[1, rows, :]) * LN2 + (jnp.log(total[0, rows, :]) - jnp.log(total[1, rows, :])))
    gaps[tp] = gap.T[:8, :]

    def gap_copy(other):
        return remote(gaps.at[tp], gaps.at[tp], g_send.at[other], g_recv.at[tp], (ctx, (tp + other) % TP))

    def gap_arrival(other):
        peer = (tp + other) % TP
        return remote(gaps.at[peer], gaps.at[peer], g_send.at[other], g_recv.at[peer], (ctx, peer))

    for other in range(1, TP):
        gap_copy(other).start()

    for m in range(2):
        for h in range(HEADS):
            rows = pl.ds(h * BLOCK, BLOCK)
            out_ref[m, :, pl.ds(h * HD, HD)] = (acc[m, rows, :] / total[m, rows, :]).astype(jnp.bfloat16)

    def wait_sends(step, _):
        m, r = step_of(step)
        for way in range(2):
            z_copy(m, r, way).wait_send()

        @pl.when(far_by_z(step))
        def _():
            for way in range(2):
                far_copy(m, r, way).wait_send()

        for kind in range(4):
            sib_copy(m, r, kind).wait_send()
        return 0

    lax.fori_loop(0, steps, wait_sends, 0)
    for m in range(2):
        for other in range(1, HALF_Y):
            @pl.when((other > row) & ((other < HALF_Y - 1) | (row == HALF_Y - 2)))
            def _():
                up_copy(m, other).wait_send()

        for r in range(2):
            @pl.when(row == HALF_Y - 2)
            def _():
                up_relay(m, r).wait_send()

        @pl.when(sends_far_up)
        def _():
            far_up(m).wait_send()

    for other in range(1, TP):
        gap_arrival(other).wait_recv()
    whole = gaps[0]
    for peer in range(1, TP):
        whole = whole + gaps[peer]
    lse_ref[...] = whole[:1, :] * (1.0 / QH)
    for other in range(1, TP):
        gap_copy(other).wait_send()


def per_device(queries, keys, values, doc_lengths):
    dma = pltpu.SemaphoreType.DMA
    attended, gap = pl.pallas_call(
        kernel,
        out_shape=[
            pltpu.VMEM((2, BLOCK, HEADS * HD), jnp.bfloat16),
            pltpu.VMEM((1, BLOCK), jnp.float32),
        ],
        in_specs=[pl.BlockSpec(memory_space=pl.ANY)] * 3 + [pl.BlockSpec(memory_space=pltpu.SMEM)],
        out_specs=[pl.BlockSpec(memory_space=pltpu.VMEM)] * 2,
        scratch_shapes=[
            pltpu.VMEM((2, HALF_Y, 2, Z_LO, CORES, BLOCK, HD), jnp.bfloat16),
            pltpu.VMEM((2, BLOCK, HEADS * HD), jnp.bfloat16),
            pltpu.VMEM((2, HEADS * BLOCK, HD), jnp.float32),
            pltpu.VMEM((2, HEADS * BLOCK, 128), jnp.float32),
            pltpu.VMEM((2, HEADS * BLOCK, 128), jnp.float32),
            pltpu.VMEM((HALF_Y, ROW_KEYS, BLOCK), jnp.bfloat16),
            pltpu.VMEM((BLOCK, BLOCK), jnp.bfloat16),
            pltpu.VMEM((TILE, ROW_KEYS), jnp.float32),
            pltpu.VMEM((TILE, ROW_KEYS), jnp.float32),
            pltpu.VMEM((TILE, ROW_KEYS), jnp.bfloat16),
            pltpu.VMEM((TILE, ROW_KEYS), jnp.bfloat16),
            pltpu.VMEM((TILE, 128), jnp.float32),
            pltpu.VMEM((TILE, 128), jnp.float32),
            pltpu.VMEM((TP, 8, 128), jnp.float32),
            dma((2, 3)),
            dma((2, HALF_Y)),
            dma((2, HALF_Y)),
            dma((2, HALF_Y, 2)),
            dma((2, HALF_Y, 2)),
            dma((2, HALF_Y, 2)),
            dma((2, HALF_Y, 2)),
            dma((2, HALF_Y, 4)),
            dma((2, HALF_Y, 4)),
            dma((2,)),
            dma((2, HALF_Y)),
            dma((TP,)),
            dma((TP,)),
        ],
        compiler_params=pltpu.CompilerParams(
            collective_id=0, has_side_effects=True, vmem_limit_bytes=60 * 2**20
        ),
        name="packed_attention",
    )(queries, keys, values, doc_lengths)
    return attended, gap.reshape(BLOCK)


def solution(mesh):
    in_specs = (P(None, "ctx", "tp"), P(None, "ctx", None), P(None, "ctx", None), P())
    out_specs = (P(None, "ctx", "tp"), P("ctx"))
    return jax.shard_map(
        per_device, mesh=mesh, in_specs=in_specs, out_specs=out_specs, check_vma=False
    )
```

```python
import functools

import jax
import jax.numpy as jnp
from jax import lax
from jax.experimental import pallas as pl
from jax.experimental.pallas import tpu as pltpu
from jax.sharding import PartitionSpec as P

QH = 64
KVH = 4
HD = 128
TOKENS = 8192
MOST = 4096
NDOCS = 16

ROWS_Y = 8
HALF_Y = 4
Z_LO = 4
CORES = 2
Z_HI = 2
TP = 8
BLOCK = 128
ROW_KEYS = Z_LO * CORES * BLOCK
HEADS = QH // TP
TILE = 256

LOG2E = 1.4426950408889634
LN2 = 0.6931471805599453
LOG2_SCALE = HD**-0.5 * LOG2E
MASKED = -1e30
EMPTY = -1e35
MESH = pl.DeviceIdType.MESH


def kernel(
    q_hbm, k_hbm, v_hbm, doc_ref, out_ref, lse_ref,
    kv, q_vm, acc, peak, total, bias, eye, scores_0, scores_1, weights_0, weights_1, factor_0, factor_1, gaps,
    load_sem, y_send, y_recv, z_send, z_recv, s_send, s_recv, u_send, g_send, g_recv,
):
    ctx = lax.axis_index("ctx")
    tp = lax.axis_index("tp")
    y = ctx // (Z_LO * CORES)
    z_lo = (ctx // CORES) % Z_LO
    core = ctx % CORES
    x = tp // Z_HI
    z = (tp % Z_HI) * Z_LO + z_lo
    half = y // HALF_Y
    row = y % HALF_Y
    steps = 2 * (row + 1)

    def at_z(where):
        where = (where + 2 * Z_HI * Z_LO) % (Z_HI * Z_LO)
        return (y * (Z_LO * CORES) + (where % Z_LO) * CORES + core, x * Z_HI + where // Z_LO)

    def at_row(where):
        return ((half * HALF_Y + where) * (Z_LO * CORES) + z_lo * CORES + core, tp)

    above, below = at_z(z + 1), at_z(z - 1)
    sibling = (ctx + 1 - 2 * core, tp)
    z_far = (z_lo + 2) % Z_LO

    barrier = pltpu.get_barrier_semaphore()

    def greet(device):
        pl.semaphore_signal(barrier, inc=1, device_id=device, device_id_type=MESH)

    greet(above)
    greet(below)
    greet(at_z(z + 2))
    greet(at_z(z - 2))
    greet(sibling)
    for other in range(1, HALF_Y):
        greet(at_row((row + other) % HALF_Y))
    for other in range(1, TP):
        greet((ctx, (tp + other) % TP))

    head = pl.ds(pl.multiple_of(x * HD, HD), HD)
    loads = []
    for m in range(2):
        loads.append(pltpu.make_async_copy(k_hbm.at[m, :, head], kv.at[m, row, 0, z_lo, core], load_sem.at[m, 0]))
        loads.append(pltpu.make_async_copy(v_hbm.at[m, :, head], kv.at[m, row, 1, z_lo, core], load_sem.at[m, 1]))
    for m in range(2):
        loads.append(pltpu.make_async_copy(q_hbm.at[m], q_vm.at[m], load_sem.at[m, 2]))
    for load in loads:
        load.start()

    position = ctx * BLOCK + lax.broadcasted_iota(jnp.int32, (8, BLOCK), 1)
    begin = jnp.zeros((8, BLOCK), jnp.int32)
    end = jnp.int32(0)
    for doc in range(NDOCS):
        end = end + doc_ref[doc]
        begin = jnp.where(position >= end, end, begin)

    for load in loads[:4]:
        load.wait()
    pl.semaphore_wait(barrier, 5 + (HALF_Y - 1) + (TP - 1))

    def step_of(step):
        return step % 2, row - step // 2

    def remote(src, dst, send, recv, device):
        return pltpu.make_async_remote_copy(
            src_ref=src, dst_ref=dst, send_sem=send, recv_sem=recv, device_id=device, device_id_type=MESH
        )

    def up_copy(m, other):
        mine = kv.at[m, row, :, z_lo, core]
        return remote(mine, mine, y_send.at[m, other], y_recv.at[m, row], at_row(other))

    def up_relay(m, r):
        block = kv.at[m, r, :, z_lo, core]
        return remote(block, block, y_send.at[m, r], y_recv.at[m, r], at_row(HALF_Y - 1))

    def from_row(m, r):
        block = kv.at[m, r, :, z_lo, core]
        return remote(block, block, y_send.at[m, 0], y_recv.at[m, r], at_row(r))

    def z_copy(m, r, way):
        block = kv.at[m, r, :, z_lo, core]
        return remote(block, block, z_send.at[m, r, way], z_recv.at[m, r], below if way else above)

    def far_copy(m, r, way):
        block = kv.at[m, r, way, z_lo, core]
        return remote(block, block, z_send.at[m, r, 2 + way], z_recv.at[m, r], at_z(z - 2 if way else z + 2))

    def arrival(m, r):
        three = kv.at[m, r, :, pl.ds(0, Z_LO - 1), core]
        return remote(three, three, z_send.at[m, r, 0], z_recv.at[m, r], above)

    def far_up(m):
        block = kv.at[m, row, :, z_far, core]
        return remote(block, block, u_send.at[m], z_recv.at[m, row], at_row(HALF_Y - 1))

    def sib_copy(m, r):
        mine = kv.at[m, r, :, :, core]
        return remote(mine, mine, s_send.at[m, r], s_recv.at[m, r], sibling)

    def sib_arrival(m, r):
        other = kv.at[m, r, :, :, 1 - core]
        return remote(other, other, s_send.at[m, r], s_recv.at[m, r], sibling)

    top_row = row == HALF_Y - 1
    sends_far_up = row < HALF_Y - 2

    def far_by_z(step):
        return jnp.logical_not(top_row & (step >= 4))

    def pass_on(m, r):
        for way in range(2):
            z_copy(m, r, way).start()

    def spread(step):
        m, r = step_of(step)
        from_row(m, r).wait_recv()
        pass_on(m, r)

        @pl.when(row == HALF_Y - 2)
        def _():
            up_relay(m, r).start()

        @pl.when(far_by_z(step))
        def _():
            for way in range(2):
                far_copy(m, r, way).start()

    def arrive(step):
        m, r = step_of(step)
        arrival(m, r).wait_recv()
        sib_copy(m, r).start()

        @pl.when(sends_far_up & (step < 2))
        def _():
            far_up(m).start()

    def gather_done(step):
        m, r = step_of(step)
        sib_arrival(m, r).wait_recv()

    pairs = HEADS * BLOCK // TILE // 2
    tile_heads = TILE // BLOCK
    scores, weights, factors = (scores_0, scores_1), (weights_0, weights_1), (factor_0, factor_1)

    def place(tile):
        tile = jnp.maximum(tile, 0)
        m, r = step_of(tile // (2 * pairs))
        return m, r, tile % (2 * pairs)

    def score(tile, slot):
        m, r, at = place(tile)
        heads = [
            q_vm[m, :, pl.ds(pl.multiple_of((at * tile_heads + h) * HD, HD), HD)] for h in range(tile_heads)
        ]
        q = jnp.concatenate([jnp.concatenate([h, eye[...]], axis=1) for h in heads], axis=0)
        keys = jnp.concatenate([kv[m, r, 0].reshape(ROW_KEYS, HD), bias[r]], axis=1)
        scores[slot][...] = lax.dot_general(q, keys, (((1,), (1,)), ((), ())), preferred_element_type=jnp.float32)

    def weigh(tile, slot):
        m, r, at = place(tile)
        rows = pl.ds(pl.multiple_of(at * TILE, TILE), TILE)
        here = scores[slot][...]
        old = peak[m, rows, :]
        new = jnp.maximum(old, jnp.max(here, axis=1, keepdims=True) * LOG2_SCALE)
        factors[slot][...] = jnp.exp2(old - new)
        peak[m, rows, :] = new
        weights[slot][...] = jnp.exp2(here * LOG2_SCALE - new[:, :1]).astype(jnp.bfloat16)

    def gather(tile, slot):
        m, r, at = place(tile)
        rows = pl.ds(pl.multiple_of(at * TILE, TILE), TILE)
        values = jnp.concatenate([kv[m, r, 1].reshape(ROW_KEYS, HD), jnp.ones((ROW_KEYS, 128), jnp.bfloat16)], axis=1)
        both = jnp.dot(weights[slot][...], values, preferred_element_type=jnp.float32)
        acc[m, rows, :] = acc[m, rows, :] * factors[slot][...] + both[:, :HD]
        total[m, rows, :] = total[m, rows, :] * factors[slot][...] + both[:, HD:]

    def mask_row(r, _):
        key_at = (half * HALF_Y + r) * ROW_KEYS + lax.broadcasted_iota(jnp.int32, (ROW_KEYS, BLOCK), 0)
        visible = (key_at >= begin[:1, :]) & (key_at <= position[:1, :])
        bias[r] = jnp.where(visible, 0.0, MASKED).astype(jnp.bfloat16)
        return 0

    def when_live(step, act):
        @pl.when(step < steps)
        def _():
            act(step)

    def when_live_after_own(step, act):
        @pl.when((step >= 4) & (step < steps))
        def _():
            act(step)

    def up(m, other):
        @pl.when(other < HALF_Y)
        def _():
            up_copy(m, other).start()

    def open_row(m):
        pass_on(m, row)
        for way in range(2):
            far_copy(m, row, way).start()

    open_row(0)
    up(0, row + 1)
    up(1, row + 1)

    acc[...] = jnp.zeros_like(acc)
    total[...] = jnp.zeros_like(total)
    peak[...] = jnp.full_like(peak, MASKED)
    scores_1[...] = jnp.full_like(scores_1, EMPTY)
    for ref in (weights_0, weights_1):
        ref[...] = jnp.zeros_like(ref)
    for ref in (factor_0, factor_1):
        ref[...] = jnp.ones_like(ref)
    eye[...] = (
        lax.broadcasted_iota(jnp.int32, (BLOCK, BLOCK), 0) == lax.broadcasted_iota(jnp.int32, (BLOCK, BLOCK), 1)
    ).astype(jnp.bfloat16)

    for m in range(2):
        @pl.when(row == 0)
        def _():
            up(m, HALF_Y - 2)

    open_row(1)
    lax.fori_loop(0, row + 1, mask_row, 0)
    when_live(2, spread)
    arrive(0)
    when_live(3, spread)

    for load in loads[4:]:
        load.wait()

    def two_tiles(tile):
        score(tile, 0)
        weigh(tile - 1, 1)
        gather(tile - 2, 0)
        score(tile + 1, 1)
        weigh(tile, 0)
        gather(tile - 1, 1)

    def whole_step(step, _):
        gather_done(step)
        when_live_after_own(step + 3, spread)
        two_tiles(2 * pairs * step)
        when_live(step + 1, arrive)
        two_tiles(2 * pairs * step + 2)
        return 0

    lax.fori_loop(0, steps, whole_step, 0)
    tiles = 2 * pairs * steps
    weigh(tiles - 1, 1)
    gather(tiles - 2, 0)
    gather(tiles - 1, 1)

    gap = jnp.zeros((BLOCK, 128), jnp.float32)
    for h in range(HEADS):
        rows = pl.ds(h * BLOCK, BLOCK)
        gap = gap + ((peak[0, rows, :] - peak[1, rows, :]) * LN2 + (jnp.log(total[0, rows, :]) - jnp.log(total[1, rows, :])))
    gaps[tp] = gap.T[:8, :]

    def gap_copy(other):
        return remote(gaps.at[tp], gaps.at[tp], g_send.at[other], g_recv.at[tp], (ctx, (tp + other) % TP))

    def gap_arrival(other):
        peer = (tp + other) % TP
        return remote(gaps.at[peer], gaps.at[peer], g_send.at[other], g_recv.at[peer], (ctx, peer))

    for other in range(1, TP):
        gap_copy(other).start()

    for m in range(2):
        for h in range(HEADS):
            rows = pl.ds(h * BLOCK, BLOCK)
            out_ref[m, :, pl.ds(h * HD, HD)] = (acc[m, rows, :] / total[m, rows, :]).astype(jnp.bfloat16)

    def wait_sends(step, _):
        m, r = step_of(step)
        for way in range(2):
            z_copy(m, r, way).wait_send()
        sib_copy(m, r).wait_send()

        @pl.when(far_by_z(step))
        def _():
            for way in range(2):
                far_copy(m, r, way).wait_send()

        return 0

    lax.fori_loop(0, steps, wait_sends, 0)
    for m in range(2):
        for other in range(1, HALF_Y):
            @pl.when((other > row) & ((other < HALF_Y - 1) | (row == HALF_Y - 2)))
            def _():
                up_copy(m, other).wait_send()

        for r in range(2):
            @pl.when(row == HALF_Y - 2)
            def _():
                up_relay(m, r).wait_send()

        @pl.when(sends_far_up)
        def _():
            far_up(m).wait_send()

    for other in range(1, TP):
        gap_arrival(other).wait_recv()
    whole = gaps[0]
    for peer in range(1, TP):
        whole = whole + gaps[peer]
    lse_ref[...] = whole[:1, :] * (1.0 / QH)
    for other in range(1, TP):
        gap_copy(other).wait_send()


def per_device(queries, keys, values, doc_lengths):
    dma = pltpu.SemaphoreType.DMA
    attended, gap = pl.pallas_call(
        kernel,
        out_shape=[
            pltpu.VMEM((2, BLOCK, HEADS * HD), jnp.bfloat16),
            pltpu.VMEM((1, BLOCK), jnp.float32),
        ],
        in_specs=[pl.BlockSpec(memory_space=pl.ANY)] * 3 + [pl.BlockSpec(memory_space=pltpu.SMEM)],
        out_specs=[pl.BlockSpec(memory_space=pltpu.VMEM)] * 2,
        scratch_shapes=[
            pltpu.VMEM((2, HALF_Y, 2, Z_LO, CORES, BLOCK, HD), jnp.bfloat16),
            pltpu.VMEM((2, BLOCK, HEADS * HD), jnp.bfloat16),
            pltpu.VMEM((2, HEADS * BLOCK, HD), jnp.float32),
            pltpu.VMEM((2, HEADS * BLOCK, 128), jnp.float32),
            pltpu.VMEM((2, HEADS * BLOCK, 128), jnp.float32),
            pltpu.VMEM((HALF_Y, ROW_KEYS, BLOCK), jnp.bfloat16),
            pltpu.VMEM((BLOCK, BLOCK), jnp.bfloat16),
            pltpu.VMEM((TILE, ROW_KEYS), jnp.float32),
            pltpu.VMEM((TILE, ROW_KEYS), jnp.float32),
            pltpu.VMEM((TILE, ROW_KEYS), jnp.bfloat16),
            pltpu.VMEM((TILE, ROW_KEYS), jnp.bfloat16),
            pltpu.VMEM((TILE, 128), jnp.float32),
            pltpu.VMEM((TILE, 128), jnp.float32),
            pltpu.VMEM((TP, 8, 128), jnp.float32),
            dma((2, 3)),
            dma((2, HALF_Y)),
            dma((2, HALF_Y)),
            dma((2, HALF_Y, 4)),
            dma((2, HALF_Y)),
            dma((2, HALF_Y)),
            dma((2, HALF_Y)),
            dma((2,)),
            dma((TP,)),
            dma((TP,)),
        ],
        compiler_params=pltpu.CompilerParams(
            collective_id=0, has_side_effects=True, vmem_limit_bytes=60 * 2**20
        ),
        name="packed_attention",
    )(queries, keys, values, doc_lengths)
    return attended, gap.reshape(BLOCK)


def solution(mesh):
    in_specs = (P(None, "ctx", "tp"), P(None, "ctx", None), P(None, "ctx", None), P())
    out_specs = (P(None, "ctx", "tp"), P("ctx"))
    return jax.shard_map(
        per_device, mesh=mesh, in_specs=in_specs, out_specs=out_specs, check_vma=False
    )
```

```python
import functools

import jax
import jax.numpy as jnp
from jax import lax
from jax.experimental import pallas as pl
from jax.experimental.pallas import tpu as pltpu
from jax.sharding import PartitionSpec as P

QH = 64
KVH = 4
HD = 128
TOKENS = 8192
MOST = 4096
NDOCS = 16

ROWS_Y = 8
HALF_Y = 4
Z_LO = 4
CORES = 2
Z_HI = 2
TP = 8
BLOCK = 128
ROW_KEYS = Z_LO * CORES * BLOCK
HEADS = QH // TP
TILE = 256

LOG2E = 1.4426950408889634
LN2 = 0.6931471805599453
LOG2_SCALE = HD**-0.5 * LOG2E
MASKED = -1e30
EMPTY = -1e35
MESH = pl.DeviceIdType.MESH


def kernel(
    q_hbm, k_hbm, v_hbm, doc_ref, out_ref, lse_ref,
    kv, q_vm, acc, peak, total, bias, eye, scores_0, scores_1, weights_0, weights_1, factor_0, factor_1, gaps,
    load_sem, y_send, y_recv, z_send, z_recv, s_send, s_recv, u_send, g_send, g_recv,
):
    ctx = lax.axis_index("ctx")
    tp = lax.axis_index("tp")
    y = ctx // (Z_LO * CORES)
    z_lo = (ctx // CORES) % Z_LO
    core = ctx % CORES
    x = tp // Z_HI
    z = (tp % Z_HI) * Z_LO + z_lo
    half = y // HALF_Y
    row = y % HALF_Y
    steps = 2 * (row + 1)

    def at_z(where):
        where = (where + 2 * Z_HI * Z_LO) % (Z_HI * Z_LO)
        return (y * (Z_LO * CORES) + (where % Z_LO) * CORES + core, x * Z_HI + where // Z_LO)

    def at_row(where):
        return ((half * HALF_Y + where) * (Z_LO * CORES) + z_lo * CORES + core, tp)

    above, below = at_z(z + 1), at_z(z - 1)
    sibling = (ctx + 1 - 2 * core, tp)
    z_far = (z_lo + 2) % Z_LO

    barrier = pltpu.get_barrier_semaphore()

    def greet(device):
        pl.semaphore_signal(barrier, inc=1, device_id=device, device_id_type=MESH)

    greet(above)
    greet(below)
    greet(at_z(z + 2))
    greet(at_z(z - 2))
    greet(sibling)
    for other in range(1, HALF_Y):
        greet(at_row((row + other) % HALF_Y))
    for other in range(1, TP):
        greet((ctx, (tp + other) % TP))

    head = pl.ds(pl.multiple_of(x * HD, HD), HD)
    loads = []
    for m in range(2):
        loads.append(pltpu.make_async_copy(k_hbm.at[m, :, head], kv.at[m, row, 0, z_lo, core], load_sem.at[m, 0]))
        loads.append(pltpu.make_async_copy(v_hbm.at[m, :, head], kv.at[m, row, 1, z_lo, core], load_sem.at[m, 1]))
    for m in range(2):
        loads.append(pltpu.make_async_copy(q_hbm.at[m], q_vm.at[m], load_sem.at[m, 2]))
    for load in loads:
        load.start()

    position = ctx * BLOCK + lax.broadcasted_iota(jnp.int32, (8, BLOCK), 1)
    begin = jnp.zeros((8, BLOCK), jnp.int32)
    end = jnp.int32(0)
    for doc in range(NDOCS):
        end = end + doc_ref[doc]
        begin = jnp.where(position >= end, end, begin)

    for load in loads[:4]:
        load.wait()
    pl.semaphore_wait(barrier, 5 + (HALF_Y - 1) + (TP - 1))

    def step_of(step):
        return step % 2, row - step // 2

    def remote(src, dst, send, recv, device):
        return pltpu.make_async_remote_copy(
            src_ref=src, dst_ref=dst, send_sem=send, recv_sem=recv, device_id=device, device_id_type=MESH
        )

    def up_copy(m, other):
        mine = kv.at[m, row, :, z_lo, core]
        return remote(mine, mine, y_send.at[m, other], y_recv.at[m, row], at_row(other))

    def up_relay(m, r):
        block = kv.at[m, r, :, z_lo, core]
        return remote(block, block, y_send.at[m, r], y_recv.at[m, r], at_row(HALF_Y - 1))

    def from_row(m, r):
        block = kv.at[m, r, :, z_lo, core]
        return remote(block, block, y_send.at[m, 0], y_recv.at[m, r], at_row(r))

    def z_copy(m, r, way):
        block = kv.at[m, r, :, z_lo, core]
        return remote(block, block, z_send.at[m, r, way], z_recv.at[m, r], below if way else above)

    def far_copy(m, r, way):
        block = kv.at[m, r, way, z_lo, core]
        return remote(block, block, z_send.at[m, r, 2 + way], z_recv.at[m, r], at_z(z - 2 if way else z + 2))

    def arrival(m, r):
        three = kv.at[m, r, :, pl.ds(0, Z_LO - 1), core]
        return remote(three, three, z_send.at[m, r, 0], z_recv.at[m, r], above)

    def far_up(m):
        block = kv.at[m, row, :, z_far, core]
        return remote(block, block, u_send.at[m], z_recv.at[m, row], at_row(HALF_Y - 1))

    def sib_copy(m, r):
        mine = kv.at[m, r, :, :, core]
        return remote(mine, mine, s_send.at[m, r], s_recv.at[m, r], sibling)

    def sib_arrival(m, r):
        other = kv.at[m, r, :, :, 1 - core]
        return remote(other, other, s_send.at[m, r], s_recv.at[m, r], sibling)

    top_row = row == HALF_Y - 1
    sends_far_up = row < HALF_Y - 2

    def far_by_z(step):
        return jnp.logical_not(top_row & (step >= 4))

    def pass_on(m, r):
        for way in range(2):
            z_copy(m, r, way).start()

    def spread(step):
        m, r = step_of(step)
        from_row(m, r).wait_recv()
        pass_on(m, r)

        @pl.when(row == HALF_Y - 2)
        def _():
            up_relay(m, r).start()

        @pl.when(far_by_z(step))
        def _():
            for way in range(2):
                far_copy(m, r, way).start()

    def arrive(step):
        m, r = step_of(step)
        arrival(m, r).wait_recv()
        sib_copy(m, r).start()

        @pl.when(sends_far_up & (step < 2))
        def _():
            far_up(m).start()

    def gather_done(step):
        m, r = step_of(step)
        sib_arrival(m, r).wait_recv()

    pairs = HEADS * BLOCK // TILE // 2
    tile_heads = TILE // BLOCK
    scores, weights, factors = (scores_0, scores_1), (weights_0, weights_1), (factor_0, factor_1)

    def place(tile):
        tile = jnp.maximum(tile, 0)
        m, r = step_of(tile // (2 * pairs))
        return m, r, tile % (2 * pairs)

    def score(tile, slot):
        m, r, at = place(tile)
        heads = [
            q_vm[m, :, pl.ds(pl.multiple_of((at * tile_heads + h) * HD, HD), HD)] for h in range(tile_heads)
        ]
        q = jnp.concatenate([jnp.concatenate([h, eye[...]], axis=1) for h in heads], axis=0)
        keys = jnp.concatenate([kv[m, r, 0].reshape(ROW_KEYS, HD), bias[r]], axis=1)
        scores[slot][...] = lax.dot_general(q, keys, (((1,), (1,)), ((), ())), preferred_element_type=jnp.float32)

    def weigh(tile, slot):
        m, r, at = place(tile)
        rows = pl.ds(pl.multiple_of(at * TILE, TILE), TILE)
        here = scores[slot][...]
        old = peak[m, rows, :]
        new = jnp.maximum(old, jnp.max(here, axis=1, keepdims=True) * LOG2_SCALE)
        factors[slot][...] = jnp.exp2(old - new)
        peak[m, rows, :] = new
        weights[slot][...] = jnp.exp2(here * LOG2_SCALE - new[:, :1]).astype(jnp.bfloat16)

    def gather(tile, slot):
        m, r, at = place(tile)
        rows = pl.ds(pl.multiple_of(at * TILE, TILE), TILE)
        values = jnp.concatenate([kv[m, r, 1].reshape(ROW_KEYS, HD), jnp.ones((ROW_KEYS, 128), jnp.bfloat16)], axis=1)
        both = jnp.dot(weights[slot][...], values, preferred_element_type=jnp.float32)
        acc[m, rows, :] = acc[m, rows, :] * factors[slot][...] + both[:, :HD]
        total[m, rows, :] = total[m, rows, :] * factors[slot][...] + both[:, HD:]

    def mask_row(r, _):
        key_at = (half * HALF_Y + r) * ROW_KEYS + lax.broadcasted_iota(jnp.int32, (ROW_KEYS, BLOCK), 0)
        visible = (key_at >= begin[:1, :]) & (key_at <= position[:1, :])
        bias[r] = jnp.where(visible, 0.0, MASKED).astype(jnp.bfloat16)
        return 0

    def when_live(step, act):
        @pl.when(step < steps)
        def _():
            act(step)

    def when_live_after_own(step, act):
        @pl.when((step >= 4) & (step < steps))
        def _():
            act(step)

    def up(m, other):
        @pl.when(other < HALF_Y)
        def _():
            up_copy(m, other).start()

    def open_row(m):
        pass_on(m, row)
        for way in range(2):
            far_copy(m, row, way).start()

    open_row(0)
    up(0, row + 1)
    up(1, row + 1)

    acc[...] = jnp.zeros_like(acc)
    total[...] = jnp.zeros_like(total)
    peak[...] = jnp.full_like(peak, MASKED)
    scores_1[...] = jnp.full_like(scores_1, EMPTY)
    for ref in (weights_0, weights_1):
        ref[...] = jnp.zeros_like(ref)
    for ref in (factor_0, factor_1):
        ref[...] = jnp.ones_like(ref)
    eye[...] = (
        lax.broadcasted_iota(jnp.int32, (BLOCK, BLOCK), 0) == lax.broadcasted_iota(jnp.int32, (BLOCK, BLOCK), 1)
    ).astype(jnp.bfloat16)

    for m in range(2):
        @pl.when(row == 0)
        def _():
            up(m, HALF_Y - 2)

    open_row(1)
    lax.fori_loop(0, row + 1, mask_row, 0)
    when_live(2, spread)
    arrive(0)
    when_live(3, spread)

    for load in loads[4:]:
        load.wait()

    def two_tiles(tile):
        score(tile, 0)
        weigh(tile - 1, 1)
        gather(tile - 2, 0)
        score(tile + 1, 1)
        weigh(tile, 0)
        gather(tile - 1, 1)

    def whole_step(step, _):
        gather_done(step)
        two_tiles(2 * pairs * step)
        when_live(step + 1, arrive)
        when_live_after_own(step + 3, spread)
        two_tiles(2 * pairs * step + 2)
        return 0

    lax.fori_loop(0, steps, whole_step, 0)
    tiles = 2 * pairs * steps
    weigh(tiles - 1, 1)
    gather(tiles - 2, 0)
    gather(tiles - 1, 1)

    gap = jnp.zeros((BLOCK, 128), jnp.float32)
    for h in range(HEADS):
        rows = pl.ds(h * BLOCK, BLOCK)
        gap = gap + ((peak[0, rows, :] - peak[1, rows, :]) * LN2 + (jnp.log(total[0, rows, :]) - jnp.log(total[1, rows, :])))
    gaps[tp] = gap.T[:8, :]

    def gap_copy(other):
        return remote(gaps.at[tp], gaps.at[tp], g_send.at[other], g_recv.at[tp], (ctx, (tp + other) % TP))

    def gap_arrival(other):
        peer = (tp + other) % TP
        return remote(gaps.at[peer], gaps.at[peer], g_send.at[other], g_recv.at[peer], (ctx, peer))

    for other in range(1, TP):
        gap_copy(other).start()

    for m in range(2):
        for h in range(HEADS):
            rows = pl.ds(h * BLOCK, BLOCK)
            out_ref[m, :, pl.ds(h * HD, HD)] = (acc[m, rows, :] / total[m, rows, :]).astype(jnp.bfloat16)

    def wait_sends(step, _):
        m, r = step_of(step)
        for way in range(2):
            z_copy(m, r, way).wait_send()
        sib_copy(m, r).wait_send()

        @pl.when(far_by_z(step))
        def _():
            for way in range(2):
                far_copy(m, r, way).wait_send()

        return 0

    lax.fori_loop(0, steps, wait_sends, 0)
    for m in range(2):
        for other in range(1, HALF_Y):
            @pl.when((other > row) & ((other < HALF_Y - 1) | (row == HALF_Y - 2)))
            def _():
                up_copy(m, other).wait_send()

        for r in range(2):
            @pl.when(row == HALF_Y - 2)
            def _():
                up_relay(m, r).wait_send()

        @pl.when(sends_far_up)
        def _():
            far_up(m).wait_send()

    for other in range(1, TP):
        gap_arrival(other).wait_recv()
    whole = gaps[0]
    for peer in range(1, TP):
        whole = whole + gaps[peer]
    lse_ref[...] = whole[:1, :] * (1.0 / QH)
    for other in range(1, TP):
        gap_copy(other).wait_send()


def per_device(queries, keys, values, doc_lengths):
    dma = pltpu.SemaphoreType.DMA
    attended, gap = pl.pallas_call(
        kernel,
        out_shape=[
            pltpu.VMEM((2, BLOCK, HEADS * HD), jnp.bfloat16),
            pltpu.VMEM((1, BLOCK), jnp.float32),
        ],
        in_specs=[pl.BlockSpec(memory_space=pl.ANY)] * 3 + [pl.BlockSpec(memory_space=pltpu.SMEM)],
        out_specs=[pl.BlockSpec(memory_space=pltpu.VMEM)] * 2,
        scratch_shapes=[
            pltpu.VMEM((2, HALF_Y, 2, Z_LO, CORES, BLOCK, HD), jnp.bfloat16),
            pltpu.VMEM((2, BLOCK, HEADS * HD), jnp.bfloat16),
            pltpu.VMEM((2, HEADS * BLOCK, HD), jnp.float32),
            pltpu.VMEM((2, HEADS * BLOCK, 128), jnp.float32),
            pltpu.VMEM((2, HEADS * BLOCK, 128), jnp.float32),
            pltpu.VMEM((HALF_Y, ROW_KEYS, BLOCK), jnp.bfloat16),
            pltpu.VMEM((BLOCK, BLOCK), jnp.bfloat16),
            pltpu.VMEM((TILE, ROW_KEYS), jnp.float32),
            pltpu.VMEM((TILE, ROW_KEYS), jnp.float32),
            pltpu.VMEM((TILE, ROW_KEYS), jnp.bfloat16),
            pltpu.VMEM((TILE, ROW_KEYS), jnp.bfloat16),
            pltpu.VMEM((TILE, 128), jnp.float32),
            pltpu.VMEM((TILE, 128), jnp.float32),
            pltpu.VMEM((TP, 8, 128), jnp.float32),
            dma((2, 3)),
            dma((2, HALF_Y)),
            dma((2, HALF_Y)),
            dma((2, HALF_Y, 4)),
            dma((2, HALF_Y)),
            dma((2, HALF_Y)),
            dma((2, HALF_Y)),
            dma((2,)),
            dma((TP,)),
            dma((TP,)),
        ],
        compiler_params=pltpu.CompilerParams(
            collective_id=0, has_side_effects=True, vmem_limit_bytes=60 * 2**20
        ),
        name="packed_attention",
    )(queries, keys, values, doc_lengths)
    return attended, gap.reshape(BLOCK)


def solution(mesh):
    in_specs = (P(None, "ctx", "tp"), P(None, "ctx", None), P(None, "ctx", None), P())
    out_specs = (P(None, "ctx", "tp"), P("ctx"))
    return jax.shard_map(
        per_device, mesh=mesh, in_specs=in_specs, out_specs=out_specs, check_vma=False
    )
```

```python
import functools

import jax
import jax.numpy as jnp
from jax import lax
from jax.experimental import pallas as pl
from jax.experimental.pallas import tpu as pltpu
from jax.sharding import PartitionSpec as P

QH = 64
KVH = 4
HD = 128
TOKENS = 8192
MOST = 4096
NDOCS = 16

ROWS_Y = 8
HALF_Y = 4
Z_LO = 4
CORES = 2
Z_HI = 2
TP = 8
BLOCK = 128
ROW_KEYS = Z_LO * CORES * BLOCK
HEADS = QH // TP
TILE = 256

LOG2E = 1.4426950408889634
LN2 = 0.6931471805599453
LOG2_SCALE = HD**-0.5 * LOG2E
MASKED = -1e30
EMPTY = -1e35
FAR_FIRST = (5, 3, 1, 7, 4, 2, 6)
MESH = pl.DeviceIdType.MESH


def kernel(
    q_hbm, k_hbm, v_hbm, doc_ref, out_ref, lse_ref,
    kv, q_vm, acc, peak, total, bias, eye, scores_0, scores_1, weights_0, weights_1, factor_0, factor_1, gaps,
    load_sem, y_send, y_recv, z_send, z_recv, s_send, s_recv, u_send, g_send, g_recv,
):
    ctx = lax.axis_index("ctx")
    tp = lax.axis_index("tp")
    y = ctx // (Z_LO * CORES)
    z_lo = (ctx // CORES) % Z_LO
    core = ctx % CORES
    x = tp // Z_HI
    z = (tp % Z_HI) * Z_LO + z_lo
    half = y // HALF_Y
    row = y % HALF_Y
    steps = 2 * (row + 1)

    def at_z(where):
        where = (where + 2 * Z_HI * Z_LO) % (Z_HI * Z_LO)
        return (y * (Z_LO * CORES) + (where % Z_LO) * CORES + core, x * Z_HI + where // Z_LO)

    def at_row(where):
        return ((half * HALF_Y + where) * (Z_LO * CORES) + z_lo * CORES + core, tp)

    above, below = at_z(z + 1), at_z(z - 1)
    sibling = (ctx + 1 - 2 * core, tp)
    z_far = (z_lo + 2) % Z_LO

    barrier = pltpu.get_barrier_semaphore()

    def greet(device):
        pl.semaphore_signal(barrier, inc=1, device_id=device, device_id_type=MESH)

    for other in FAR_FIRST:
        greet((ctx, (tp + other) % TP))
    greet(above)
    greet(below)
    greet(at_z(z + 2))
    greet(at_z(z - 2))
    greet(sibling)
    for other in range(1, HALF_Y):
        greet(at_row((row + other) % HALF_Y))

    head = pl.ds(pl.multiple_of(x * HD, HD), HD)
    loads = []
    for m in range(2):
        loads.append(pltpu.make_async_copy(k_hbm.at[m, :, head], kv.at[m, row, 0, z_lo, core], load_sem.at[m, 0]))
        loads.append(pltpu.make_async_copy(v_hbm.at[m, :, head], kv.at[m, row, 1, z_lo, core], load_sem.at[m, 1]))
    for m in range(2):
        loads.append(pltpu.make_async_copy(q_hbm.at[m], q_vm.at[m], load_sem.at[m, 2]))
    for load in loads:
        load.start()

    position = ctx * BLOCK + lax.broadcasted_iota(jnp.int32, (8, BLOCK), 1)
    begin = jnp.zeros((8, BLOCK), jnp.int32)
    end = jnp.int32(0)
    for doc in range(NDOCS):
        end = end + doc_ref[doc]
        begin = jnp.where(position >= end, end, begin)

    for load in loads[:4]:
        load.wait()
    pl.semaphore_wait(barrier, 5 + (HALF_Y - 1) + (TP - 1))

    def step_of(step):
        return step % 2, row - step // 2

    def remote(src, dst, send, recv, device):
        return pltpu.make_async_remote_copy(
            src_ref=src, dst_ref=dst, send_sem=send, recv_sem=recv, device_id=device, device_id_type=MESH
        )

    def up_copy(m, other):
        mine = kv.at[m, row, :, z_lo, core]
        return remote(mine, mine, y_send.at[m, other], y_recv.at[m, row], at_row(other))

    def up_relay(m, r):
        block = kv.at[m, r, :, z_lo, core]
        return remote(block, block, y_send.at[m, r], y_recv.at[m, r], at_row(HALF_Y - 1))

    def from_row(m, r):
        block = kv.at[m, r, :, z_lo, core]
        return remote(block, block, y_send.at[m, 0], y_recv.at[m, r], at_row(r))

    def z_copy(m, r, way):
        block = kv.at[m, r, :, z_lo, core]
        return remote(block, block, z_send.at[m, r, way], z_recv.at[m, r], below if way else above)

    def far_copy(m, r, way):
        block = kv.at[m, r, way, z_lo, core]
        return remote(block, block, z_send.at[m, r, 2 + way], z_recv.at[m, r], at_z(z - 2 if way else z + 2))

    def arrival(m, r):
        three = kv.at[m, r, :, pl.ds(0, Z_LO - 1), core]
        return remote(three, three, z_send.at[m, r, 0], z_recv.at[m, r], above)

    def far_up(m):
        block = kv.at[m, row, :, z_far, core]
        return remote(block, block, u_send.at[m], z_recv.at[m, row], at_row(HALF_Y - 1))

    def sib_copy(m, r):
        mine = kv.at[m, r, :, :, core]
        return remote(mine, mine, s_send.at[m, r], s_recv.at[m, r], sibling)

    def sib_arrival(m, r):
        other = kv.at[m, r, :, :, 1 - core]
        return remote(other, other, s_send.at[m, r], s_recv.at[m, r], sibling)

    top_row = row == HALF_Y - 1
    sends_far_up = row < HALF_Y - 2

    def far_by_z(step):
        return jnp.logical_not(top_row & (step >= 4))

    def pass_on(m, r):
        for way in range(2):
            z_copy(m, r, way).start()

    def spread(step):
        m, r = step_of(step)
        from_row(m, r).wait_recv()
        pass_on(m, r)

        @pl.when(row == HALF_Y - 2)
        def _():
            up_relay(m, r).start()

        @pl.when(far_by_z(step))
        def _():
            for way in range(2):
                far_copy(m, r, way).start()

    def arrive(step):
        m, r = step_of(step)
        arrival(m, r).wait_recv()
        sib_copy(m, r).start()

        @pl.when(sends_far_up & (step < 2))
        def _():
            far_up(m).start()

    def gather_done(step):
        m, r = step_of(step)
        sib_arrival(m, r).wait_recv()

    pairs = HEADS * BLOCK // TILE // 2
    tile_heads = TILE // BLOCK
    scores, weights, factors = (scores_0, scores_1), (weights_0, weights_1), (factor_0, factor_1)

    def place(tile):
        tile = jnp.maximum(tile, 0)
        m, r = step_of(tile // (2 * pairs))
        return m, r, tile % (2 * pairs)

    def score(tile, slot):
        m, r, at = place(tile)
        heads = [
            q_vm[m, :, pl.ds(pl.multiple_of((at * tile_heads + h) * HD, HD), HD)] for h in range(tile_heads)
        ]
        q = jnp.concatenate([jnp.concatenate([h, eye[...]], axis=1) for h in heads], axis=0)
        keys = jnp.concatenate([kv[m, r, 0].reshape(ROW_KEYS, HD), bias[r]], axis=1)
        scores[slot][...] = lax.dot_general(q, keys, (((1,), (1,)), ((), ())), preferred_element_type=jnp.float32)

    def weigh(tile, slot):
        m, r, at = place(tile)
        rows = pl.ds(pl.multiple_of(at * TILE, TILE), TILE)
        here = scores[slot][...]
        old = peak[m, rows, :]
        new = jnp.maximum(old, jnp.max(here, axis=1, keepdims=True) * LOG2_SCALE)
        factors[slot][...] = jnp.exp2(old - new)
        peak[m, rows, :] = new
        weights[slot][...] = jnp.exp2(here * LOG2_SCALE - new[:, :1]).astype(jnp.bfloat16)

    def gather(tile, slot):
        m, r, at = place(tile)
        rows = pl.ds(pl.multiple_of(at * TILE, TILE), TILE)
        values = jnp.concatenate([kv[m, r, 1].reshape(ROW_KEYS, HD), jnp.ones((ROW_KEYS, 128), jnp.bfloat16)], axis=1)
        both = jnp.dot(weights[slot][...], values, preferred_element_type=jnp.float32)
        acc[m, rows, :] = acc[m, rows, :] * factors[slot][...] + both[:, :HD]
        total[m, rows, :] = total[m, rows, :] * factors[slot][...] + both[:, HD:]

    def mask_row(r, _):
        key_at = (half * HALF_Y + r) * ROW_KEYS + lax.broadcasted_iota(jnp.int32, (ROW_KEYS, BLOCK), 0)
        visible = (key_at >= begin[:1, :]) & (key_at <= position[:1, :])
        bias[r] = jnp.where(visible, 0.0, MASKED).astype(jnp.bfloat16)
        return 0

    def when_live(step, act):
        @pl.when(step < steps)
        def _():
            act(step)

    def when_live_after_own(step, act):
        @pl.when((step >= 4) & (step < steps))
        def _():
            act(step)

    def up(m, other):
        @pl.when(other < HALF_Y)
        def _():
            up_copy(m, other).start()

    def open_row(m):
        pass_on(m, row)
        for way in range(2):
            far_copy(m, row, way).start()

    open_row(0)
    up(0, row + 1)
    up(1, row + 1)

    acc[...] = jnp.zeros_like(acc)
    total[...] = jnp.zeros_like(total)
    peak[...] = jnp.full_like(peak, MASKED)
    scores_1[...] = jnp.full_like(scores_1, EMPTY)
    for ref in (weights_0, weights_1):
        ref[...] = jnp.zeros_like(ref)
    for ref in (factor_0, factor_1):
        ref[...] = jnp.ones_like(ref)
    eye[...] = (
        lax.broadcasted_iota(jnp.int32, (BLOCK, BLOCK), 0) == lax.broadcasted_iota(jnp.int32, (BLOCK, BLOCK), 1)
    ).astype(jnp.bfloat16)

    for m in range(2):
        @pl.when(row == 0)
        def _():
            up(m, HALF_Y - 2)

    open_row(1)
    lax.fori_loop(0, row + 1, mask_row, 0)
    when_live(2, spread)
    arrive(0)
    when_live(3, spread)

    for load in loads[4:]:
        load.wait()

    def two_tiles(tile):
        score(tile, 0)
        weigh(tile - 1, 1)
        gather(tile - 2, 0)
        score(tile + 1, 1)
        weigh(tile, 0)
        gather(tile - 1, 1)

    def whole_step(step, _):
        gather_done(step)
        two_tiles(2 * pairs * step)
        when_live(step + 1, arrive)
        when_live_after_own(step + 3, spread)
        two_tiles(2 * pairs * step + 2)
        return 0

    lax.fori_loop(0, steps, whole_step, 0)
    tiles = 2 * pairs * steps
    weigh(tiles - 1, 1)
    gather(tiles - 2, 0)
    gather(tiles - 1, 1)

    gap = jnp.zeros((BLOCK, 128), jnp.float32)
    for h in range(HEADS):
        rows = pl.ds(h * BLOCK, BLOCK)
        gap = gap + ((peak[0, rows, :] - peak[1, rows, :]) * LN2 + (jnp.log(total[0, rows, :]) - jnp.log(total[1, rows, :])))
    gaps[tp] = gap.T[:8, :]

    def gap_copy(other):
        return remote(gaps.at[tp], gaps.at[tp], g_send.at[other], g_recv.at[tp], (ctx, (tp + other) % TP))

    def gap_arrival(other):
        peer = (tp + other) % TP
        return remote(gaps.at[peer], gaps.at[peer], g_send.at[other], g_recv.at[peer], (ctx, peer))

    for other in FAR_FIRST:
        gap_copy(other).start()

    for m in range(2):
        for h in range(HEADS):
            rows = pl.ds(h * BLOCK, BLOCK)
            out_ref[m, :, pl.ds(h * HD, HD)] = (acc[m, rows, :] / total[m, rows, :]).astype(jnp.bfloat16)

    def wait_sends(step, _):
        m, r = step_of(step)
        for way in range(2):
            z_copy(m, r, way).wait_send()
        sib_copy(m, r).wait_send()

        @pl.when(far_by_z(step))
        def _():
            for way in range(2):
                far_copy(m, r, way).wait_send()

        return 0

    lax.fori_loop(0, steps, wait_sends, 0)
    for m in range(2):
        for other in range(1, HALF_Y):
            @pl.when((other > row) & ((other < HALF_Y - 1) | (row == HALF_Y - 2)))
            def _():
                up_copy(m, other).wait_send()

        for r in range(2):
            @pl.when(row == HALF_Y - 2)
            def _():
                up_relay(m, r).wait_send()

        @pl.when(sends_far_up)
        def _():
            far_up(m).wait_send()

    for other in range(1, TP):
        gap_arrival(other).wait_recv()
    whole = gaps[0]
    for peer in range(1, TP):
        whole = whole + gaps[peer]
    lse_ref[...] = whole[:1, :] * (1.0 / QH)
    for other in range(1, TP):
        gap_copy(other).wait_send()


def per_device(queries, keys, values, doc_lengths):
    dma = pltpu.SemaphoreType.DMA
    attended, gap = pl.pallas_call(
        kernel,
        out_shape=[
            pltpu.VMEM((2, BLOCK, HEADS * HD), jnp.bfloat16),
            pltpu.VMEM((1, BLOCK), jnp.float32),
        ],
        in_specs=[pl.BlockSpec(memory_space=pl.ANY)] * 3 + [pl.BlockSpec(memory_space=pltpu.SMEM)],
        out_specs=[pl.BlockSpec(memory_space=pltpu.VMEM)] * 2,
        scratch_shapes=[
            pltpu.VMEM((2, HALF_Y, 2, Z_LO, CORES, BLOCK, HD), jnp.bfloat16),
            pltpu.VMEM((2, BLOCK, HEADS * HD), jnp.bfloat16),
            pltpu.VMEM((2, HEADS * BLOCK, HD), jnp.float32),
            pltpu.VMEM((2, HEADS * BLOCK, 128), jnp.float32),
            pltpu.VMEM((2, HEADS * BLOCK, 128), jnp.float32),
            pltpu.VMEM((HALF_Y, ROW_KEYS, BLOCK), jnp.bfloat16),
            pltpu.VMEM((BLOCK, BLOCK), jnp.bfloat16),
            pltpu.VMEM((TILE, ROW_KEYS), jnp.float32),
            pltpu.VMEM((TILE, ROW_KEYS), jnp.float32),
            pltpu.VMEM((TILE, ROW_KEYS), jnp.bfloat16),
            pltpu.VMEM((TILE, ROW_KEYS), jnp.bfloat16),
            pltpu.VMEM((TILE, 128), jnp.float32),
            pltpu.VMEM((TILE, 128), jnp.float32),
            pltpu.VMEM((TP, 8, 128), jnp.float32),
            dma((2, 3)),
            dma((2, HALF_Y)),
            dma((2, HALF_Y)),
            dma((2, HALF_Y, 4)),
            dma((2, HALF_Y)),
            dma((2, HALF_Y)),
            dma((2, HALF_Y)),
            dma((2,)),
            dma((TP,)),
            dma((TP,)),
        ],
        compiler_params=pltpu.CompilerParams(
            collective_id=0, has_side_effects=True, vmem_limit_bytes=60 * 2**20
        ),
        name="packed_attention",
    )(queries, keys, values, doc_lengths)
    return attended, gap.reshape(BLOCK)


def solution(mesh):
    in_specs = (P(None, "ctx", "tp"), P(None, "ctx", None), P(None, "ctx", None), P())
    out_specs = (P(None, "ctx", "tp"), P("ctx"))
    return jax.shard_map(
        per_device, mesh=mesh, in_specs=in_specs, out_specs=out_specs, check_vma=False
    )
```
